256 devices in a mesh: atm: 32 (over x, z), ocn: 8 (over y, core).
Axes of the slice: x: 4, y: 4, z: 8, core: 2. Of those that a mesh axis runs over, the one named last changes fastest.
Arguments:
- state: bfloat16 [1048576, 256], P(('atm', 'ocn')), may hold values from -6 to 6
- branch_id: int32 [1048576], P(('atm', 'ocn')), may hold values from 0 to 1, as said below
- span_map: int32 [65536], P(('atm', 'ocn')), may hold values from 0 to 65535, as said below
- derivative: bfloat16 [16, 16], replicated, may hold values from -1.5 to 1.5
- rad_weight: bfloat16 [256, 2048], replicated, may hold values from -0.375 to 0.375
- conv_in: bfloat16 [256, 2048], replicated, may hold values from -0.375 to 0.375
- conv_out: bfloat16 [2048, 256], replicated, may hold values from -0.125 to 0.125
- flux_weight: bfloat16 [256, 4], replicated, may hold values from -0.375 to 0.375
- remap_cell: int32 [4, 1048576], P(None, ('atm', 'ocn')), may hold values from 0 to 4095
- remap_weight: float32 [4, 1048576], P(None, ('atm', 'ocn')), may hold values from 0.02 to 0.25
- ocean_state: float32 [2, 131072], P(None, ('atm', 'ocn')), may hold values from -6 to 6
- ocean_mask: int32 [131072], P(('atm', 'ocn')), may hold values 0 or 1
- couple: float32 [4, 2], replicated, may hold values from -3 to 3
Outputs:
- new_state: bfloat16 [1048576, 256], P(('atm', 'ocn'))
- span_tend: bfloat16 [1048576, 256], P(('atm', 'ocn'))
- ocean_new: float32 [2, 131072], P(None, ('atm', 'ocn'))
- surface: float32 [2, 1048576], P(None, ('atm', 'ocn'))
The draws below stay inside these ranges and needn't reach their ends.
Inputs may be any that keep to these rules, and one draw needn't show every extreme that they name: span_map is a permutation of the elements; the place span_map gives an element (a block of 16 rows in span layout) lies on a device with the same ocn index; each device keeps 256 // 2 of its elements on itself and sends exactly 8 to each of 16 other devices with its ocn index, none to the rest. `branch_id`: every physics span (the 256 elements that span_map places on one device) holds exactly 1024 columns with id 1. `remap_cell`: an index into the 4096 ocean cells of the devices with the column's atm index.
All inputs are finite; a program needn't handle non-finite values. No bound on the sum of `ocean_mask` on one device may be relied on, other than what follows from the above.
Results may differ from the reference program's by a relative error of at most 0.012.
Values may be sent and summed in bfloat16 or wider, within the bound.
A program may use at most 64 MiB of HBM per device.

```python
import jax
import jax.numpy as jnp
from jax import lax

LEV = 128
FEAT = 256
NBAND = 8
CONV_HID = 2048
NODES = 16
NFLX = 4
NSRF = 2
NNZ = 4
COLS_DEV = 4096
EL_DEV = 256
MOVE = 8
CONV_DEV = 1024
COLUMNS = 1048576
OC_GRP = 4096
OCELLS = 131072
N_ATM = 32
N_OCN = 8
DEVICES = 256


def shared_map(key):
    group_size = N_ATM * EL_DEV

    def one_section(row_key, ocn_index):
        shift_key, pick_key, order_rkey = jax.random.split(row_key, 3)
        shifts = jax.random.permutation(shift_key, N_ATM - 1)[:N_ATM // 2].astype(jnp.int32) + 1
        shift_list = jnp.concatenate([jnp.zeros((EL_DEV // 2,), jnp.int32), jnp.repeat(shifts, MOVE)])

        def per_source(k, a):
            return (a + jax.random.permutation(k, shift_list)) % N_ATM
        target = jax.vmap(per_source)(jax.random.split(pick_key, N_ATM), jnp.arange(N_ATM, dtype=jnp.int32))
        target = target.reshape(-1).astype(jnp.int32)
        order_key = jax.random.permutation(order_rkey, group_size).astype(jnp.int32)
        score = target * group_size + order_key
        sorted_at = jnp.argsort(score, stable=True).astype(jnp.int32)
        position = jnp.zeros((group_size,), jnp.int32).at[sorted_at].set(jnp.arange(group_size, dtype=jnp.int32))
        dest_slot = position - target * EL_DEV
        return ((target * N_OCN + ocn_index) * EL_DEV + dest_slot).reshape(N_ATM, EL_DEV)
    section_rows = jax.vmap(one_section)(jax.random.split(key, N_OCN), jnp.arange(N_OCN, dtype=jnp.int32))
    return jnp.transpose(section_rows, (1, 0, 2)).reshape(-1).astype(jnp.int32)


def draw_span_map(key, part):
    mapping = shared_map(key)
    return mapping


def draw_branch_id(key, part):
    mapping = shared_map(key)
    key = jax.random.fold_in(key, 11)

    def span(k):
        return (jax.random.permutation(k, COLS_DEV) < CONV_DEV).astype(jnp.int32)
    span_flags = jax.vmap(span)(jax.random.split(key, DEVICES)).reshape(-1)
    dyn_index = (mapping[:, None] * NODES + jnp.arange(NODES, dtype=jnp.int32)[None, :]).reshape(-1)
    return span_flags[dyn_index]


def with_ends(array, stream_key, least, top_value):
    spot = [jax.random.randint(jax.random.fold_in(stream_key, axis), (), 0, length) for axis, length in enumerate(array.shape)]
    main_axis = array.shape.index(max(array.shape))
    neighbour = spot[:main_axis] + [(spot[main_axis] + 1) % array.shape[main_axis]] + spot[main_axis + 1:]
    return array.at[tuple(spot)].set(least).at[tuple(neighbour)].set(top_value)


def levels(own_key, extent, cuts, least, high):
    factor_of, own = 1.0, jax.random.fold_in(own_key, 6)
    for axis_at, shards_of in cuts:
        draws = jnp.exp(jax.random.uniform(jax.random.fold_in(own, axis_at), (shards_of,), jnp.float32, least / len(cuts), high / len(cuts)))
        factor_of = factor_of * jnp.repeat(draws, extent[axis_at] // shards_of).reshape([-1 if axis == axis_at else 1 for axis in range(len(extent))])
    return factor_of


def normal_values(own_key, shape, width, most, shards=(), kind=jnp.bfloat16):
    array = jax.random.normal(own_key, shape, jnp.float32) * width
    if len(shards) > 0:
        array = levels(own_key, shape, shards, -0.22, 0.18) * array
    return jnp.clip(array, min=-most, max=most).astype(kind)


def setup_inputs(seed: int = 0) -> dict:
    keys = jax.random.split(jax.random.key(seed), 14)
    return {
        "state": normal_values(keys[0], (COLUMNS, FEAT), 1.0, 6.0, ((0, 256),)),
        "branch_id": draw_branch_id(jax.random.fold_in(keys[13], 71), 0),
        "span_map": draw_span_map(jax.random.fold_in(keys[13], 71), 0),
        "derivative": normal_values(keys[3], (NODES, NODES), 0.25, 1.5),
        "rad_weight": normal_values(keys[4], (FEAT, NBAND * FEAT), FEAT ** -0.5, 0.375),
        "conv_in": normal_values(keys[5], (FEAT, CONV_HID), FEAT ** -0.5, 0.375),
        "conv_out": normal_values(keys[6], (CONV_HID, FEAT), CONV_HID ** -0.5, 0.125),
        "flux_weight": normal_values(keys[7], (FEAT, NFLX), FEAT ** -0.5, 0.375),
        "remap_cell": with_ends(jax.random.randint(keys[8], (NNZ, COLUMNS), 0, OC_GRP), jax.random.fold_in(keys[8], 1), 0, OC_GRP - 1).astype(jnp.int32),
        "remap_weight": jnp.clip(0.02 + 0.23 * jax.random.uniform(keys[9], (NNZ, COLUMNS), jnp.float32) ** levels(keys[9], (NNZ, COLUMNS), ((1, 256),), -0.2, 0.2), 0.02, 0.25),
        "ocean_state": normal_values(keys[10], (NSRF, OCELLS), 1.0, 6.0, ((1, 256),), jnp.float32),
        "ocean_mask": with_ends((jax.random.randint(keys[11], (OCELLS,), 0, 4) < 3).astype(jnp.int32), jax.random.fold_in(keys[11], 1), 0, 1),
        "couple": normal_values(keys[12], (NFLX, NSRF), NFLX ** -0.5, 3.0, (), jnp.float32),
    }


def radiation(x, rad_weight):
    feat_width = x.shape[1]
    band_terms = jnp.dot(x, rad_weight, preferred_element_type=jnp.float32)
    band_terms = band_terms.reshape(x.shape[0], NBAND, feat_width)
    return 0.25 * jnp.sum(jnp.tanh(band_terms), axis=1)


def convection(x, conv_in, conv_out):
    hidden = jax.nn.silu(jnp.dot(x, conv_in, preferred_element_type=jnp.float32)).astype(jnp.bfloat16)
    return jnp.dot(hidden, conv_out, preferred_element_type=jnp.float32)


def reference(state, branch_id, span_map, derivative, rad_weight, conv_in, conv_out, flux_weight, remap_cell, remap_weight, ocean_state, ocean_mask, couple):
    feat_width = 2 * LEV
    deriv_f = derivative.astype(jnp.float32)

    def per_block(x):
        radiative = radiation(x, rad_weight)
        blocks = x.astype(jnp.float32).reshape(-1, NODES, feat_width)
        dynamics = jnp.einsum("ij,ejf->eif", deriv_f, blocks).reshape(-1, feat_width)
        return radiative, dynamics

    radiative, dynamics = lax.map(per_block, state.reshape(-1, COLS_DEV, feat_width))
    radiative = radiative.reshape(COLUMNS, feat_width)
    dynamics = dynamics.reshape(COLUMNS, feat_width)
    conv_rows = jnp.nonzero(branch_id == 1, size=COLUMNS // 4)[0].astype(jnp.int32)
    picked = state[conv_rows].reshape(-1, COLS_DEV, feat_width)
    convective = lax.map(lambda x: convection(x, conv_in, conv_out), picked).reshape(-1, feat_width)
    tendency = radiative.at[conv_rows].add(convective).astype(jnp.bfloat16)
    new_state = (state.astype(jnp.float32) + dynamics + tendency.astype(jnp.float32)).astype(jnp.bfloat16)
    span_index = (span_map[:, None] * NODES + jnp.arange(NODES, dtype=jnp.int32)[None, :]).reshape(-1)
    span_tend = jnp.zeros_like(tendency).at[span_index].set(tendency)
    surface_flux = jnp.dot(tendency, flux_weight, preferred_element_type=jnp.float32)
    col_group = (jnp.arange(COLUMNS, dtype=jnp.int32) // COLS_DEV) // N_OCN
    cell_index = col_group[None, :] * OC_GRP + remap_cell
    weighted = (remap_weight[:, :, None] * surface_flux[None, :, :]).reshape(-1, NFLX)
    ocean_flux = jax.ops.segment_sum(weighted, cell_index.reshape(-1), num_segments=OCELLS).T
    mask_f = ocean_mask.astype(jnp.float32)
    forcing = jnp.dot(couple.T, ocean_flux, precision=lax.Precision.HIGHEST)
    ocean_new = ocean_state + mask_f[None, :] * jnp.tanh(forcing)
    sea_values = mask_f[None, :] * ocean_new
    sea_part = jnp.sum(remap_weight[None, :, :] * sea_values[:, cell_index], axis=1)
    sea_share = jnp.sum(remap_weight * mask_f[cell_index], axis=0)
    land_values = jnp.stack([new_state[:, LEV - 1], new_state[:, 2 * LEV - 1]]).astype(jnp.float32)
    surface = sea_part + (1.0 - sea_share)[None, :] * land_values
    return new_state, span_tend, ocean_new, surface
```

```python
import jax
import jax.numpy as jnp
from jax import lax
from jax.experimental import pallas as pl
from jax.experimental.pallas import tpu as pltpu
from jax.sharding import PartitionSpec as P

MESH = pl.DeviceIdType.MESH
F32 = jnp.float32
BF16 = jnp.bfloat16
I32 = jnp.int32

NX, NZ = 4, 8
NPEER = NX * NZ - 1
NOCN = 8
NE = 256
ND = 16
NF = 256
ROWS = NE * ND
MOVE = 8
MROWS = MOVE * ND
NMOVED = NE // 2
RB = 256
EB = RB // ND
NB = ROWS // RB
NBM = NMOVED // EB
CB = 512
PLACE = 32


def iota(shape, dim):
    return lax.broadcasted_iota(I32, shape, dim)


def onehot(cond):
    return jnp.where(cond, 1.0, 0.0).astype(F32)


def dot(a, b):
    return jnp.dot(a, b, preferred_element_type=F32)


def dot_nt(a, b):
    return lax.dot_general(a, b, (((1,), (1,)), ((), ())), preferred_element_type=F32)


def column(row):
    parts = [
        jnp.broadcast_to(row[:, h * 128 : (h + 1) * 128], (128, 128)).T for h in range(2)
    ]
    half = jnp.concatenate(parts, axis=0)
    return jnp.concatenate([half, half], axis=1)


def plan_kernel(
    span_hbm, branch_hbm, deriv_hbm, scal, msg_out, mask_ord, dblk, span_ref, branch_ref, deriv_ref, sem
):
    copies = [
        pltpu.make_async_copy(src, dst, sem.at[n])
        for n, (src, dst) in enumerate(
            [(span_hbm, span_ref), (branch_hbm, branch_ref), (deriv_hbm, deriv_ref)]
        )
    ]
    for copy in copies:
        copy.start()
    atm = lax.axis_index("atm")
    x = atm // NZ
    z = lax.rem(atm, NZ)
    for copy in copies:
        copy.wait()
    span = span_ref[...]
    slot_r = (span & (NE - 1)).astype(F32)
    target = span >> 11
    rel = ((((target >> 3) - x) & (NX - 1)) << 3) + (((target & (NZ - 1)) - z) & (NZ - 1))
    key_i = jnp.where(rel == 0, NPEER, rel - 1)
    key_r = key_i.astype(F32)
    both_r = (key_i * NE + iota((1, NE), 1)).astype(F32)
    key_c = column(key_r)
    both_c = column(both_r)
    lane = iota((NE, NE), 1).astype(F32)
    sub = iota((NE, NE), 0).astype(F32)
    pos_r = jnp.sum(onehot(both_c < both_r), axis=0, keepdims=True)
    less_r = jnp.sum(onehot(key_c < key_r), axis=0, keepdims=True)
    base_r = jnp.sum(onehot(key_c < lane), axis=0, keepdims=True)
    pos_c = column(pos_r)
    src_r = jnp.sum(jnp.where(pos_c == lane, sub, 0.0), axis=0, keepdims=True)
    scal[0:1, :] = src_r.astype(I32)
    scal[1:2, :] = pos_r.astype(I32)
    scal[2:3, :] = base_r.astype(I32)
    rank_r = jnp.where(key_r == NPEER, pos_r - (NMOVED - 1), pos_r - less_r + 1.0)
    pick = jnp.where(key_r == iota((32, NE), 0).astype(F32), rank_r, 0.0).astype(BF16)
    slots = onehot(column(slot_r) == lane).astype(BF16)
    msg = dot(pick, slots)
    packed = (msg[:, :128] + 256.0 * msg[:, 128:]).astype(I32)
    for i in range(32):
        msg_out[i] = packed[i : i + 1, :]
    bits = branch_ref[...].astype(F32).astype(BF16)
    spread = dot(onehot(iota((NE, 32), 0) // 8 == iota((NE, 32), 1)).astype(BF16), bits)
    own = jnp.where(iota((NE, 128), 1) // ND == iota((NE, 128), 0) % 8, spread, 0.0)
    fold = onehot(iota((128, 128), 0) % ND == iota((128, 128), 1) % ND).astype(BF16)
    bits_nat = dot(own.astype(BF16), fold).astype(BF16)
    order = onehot(pos_r == sub).astype(BF16)
    mask_ord[...] = dot(order, bits_nat).astype(BF16)
    spread_rows = onehot(iota((RB, ND), 0) % ND == iota((RB, ND), 1)).astype(BF16)
    tiled = dot_nt(dot(spread_rows, deriv_ref[...]).astype(BF16), spread_rows)
    same = iota((RB, RB), 0) // ND == iota((RB, RB), 1) // ND
    dblk[...] = jnp.where(same, tiled, 0.0).astype(BF16)


def kernel(
    scal,
    msg_out,
    mask_ord,
    dblk,
    couple_hbm,
    fw_hbm,
    cell_hbm,
    weight_hbm,
    ostate_hbm,
    omask_hbm,
    state_hbm,
    rad_hbm,
    cin_hbm,
    cout_hbm,
    new_ref,
    pool,
    q_v,
    onew_ref,
    surf_ref,
    state,
    rad,
    cin,
    cout,
    fw_ref,
    cell_ref,
    weight_ref,
    ostate_ref,
    omask_ref,
    couple_ref,
    xs,
    ordered,
    send,
    msg_in,
    scal_s,
    flux16,
    land,
    facc,
    rs_out,
    rs_in,
    table,
    load_sem,
    dsend,
    drecv,
    msend,
    mrecv,
    rsend,
    rrecv,
    asend,
    arecv,
):
    atm = lax.axis_index("atm")
    ocn = lax.axis_index("ocn")
    x = atm // NZ
    z = lax.rem(atm, NZ)

    def peer(i):
        rel = i + 1
        return lax.rem(x + rel // NZ, NX) * NZ + lax.rem(z + lax.rem(rel, NZ), NZ)

    def sea(q):
        return lax.rem(ocn + q, NOCN)

    barrier = pltpu.get_barrier_semaphore()
    loads = [
        pltpu.make_async_copy(src, dst, load_sem.at[n])
        for n, (src, dst) in enumerate(
            [
                (state_hbm, state),
                (rad_hbm, rad),
                (cin_hbm, cin),
                (cout_hbm, cout),
                (fw_hbm, fw_ref),
                (cell_hbm, cell_ref),
                (weight_hbm, weight_ref),
                (ostate_hbm, ostate_ref),
                (omask_hbm, omask_ref),
                (couple_hbm, couple_ref),
            ]
        )
    ]
    for copy in loads:
        copy.start()

    @pl.loop(0, NPEER)
    def _(i):
        pl.semaphore_signal(barrier, inc=1, device_id=(peer(i), ocn), device_id_type=MESH)

    @pl.loop(1, NOCN)
    def _(q):
        pl.semaphore_signal(barrier, inc=1, device_id=(atm, sea(q)), device_id_type=MESH)

    scal_copy = pltpu.make_async_copy(scal, scal_s, load_sem.at[10])
    scal_copy.start()
    for copy in loads:
        copy.wait()
    scal_copy.wait()

    to_rows = onehot(iota((RB, EB), 0) // ND == iota((RB, EB), 1)).astype(BF16)
    my_lane = iota((RB, 128), 1) == iota((RB, 128), 0) % ND
    ones = jnp.ones((128, NF), BF16)

    def physics(b):
        for j in range(EB):
            at = scal_s[0, b * EB + j] * ND
            xs[j * ND : (j + 1) * ND, :] = state[pl.ds(at, ND), :]
        cols = xs[...]
        total = jnp.zeros((RB, NF), F32)
        conv = jnp.zeros((RB, NF), F32)
        for g in range(8):
            part = slice(g * NF, (g + 1) * NF)
            total += jnp.tanh(dot(cols, rad[:, part]))
            half = 0.5 * dot(cols, cin[:, part])
            hidden = (half * (1.0 + jnp.tanh(half))).astype(BF16)
            conv += dot(hidden, cout[part, :])
        bits_b = mask_ord[pl.ds(pl.multiple_of(b * EB, EB), EB), :]
        mine = jnp.where(my_lane, dot(to_rows, bits_b), 0.0).astype(BF16)
        mask = dot(mine, ones)
        out = (0.25 * total + mask * conv).astype(BF16)
        ordered[pl.ds(pl.multiple_of(b * RB, RB), RB), :] = out
        return out

    def data_copy(i):
        return pltpu.make_async_remote_copy(
            src_ref=send.at[i],
            dst_ref=pool.at[pl.ds(pl.multiple_of(i * MROWS, MROWS), MROWS)],
            send_sem=dsend.at[i],
            recv_sem=drecv.at[i],
            device_id=(peer(i), ocn),
            device_id_type=MESH,
        )

    def msg_copy(i):
        return pltpu.make_async_remote_copy(
            src_ref=msg_out.at[i],
            dst_ref=msg_in.at[i],
            send_sem=msend.at[i],
            recv_sem=mrecv.at[i],
            device_id=(peer(i), ocn),
            device_id_type=MESH,
        )

    def ship(i):
        at = scal_s[2, i] * ND
        send[i] = ordered[pl.ds(at, MROWS), :]
        msg_copy(i).start()
        data_copy(i).start()

    per_block = EB // MOVE
    physics(0)
    pl.semaphore_wait(barrier, NPEER + NOCN - 1)
    for i in range(per_block):
        ship(i)

    @pl.loop(1, NBM)
    def _(b):
        physics(b)
        for i in range(per_block):
            ship(b * per_block + i)

    @pl.loop(NBM * per_block, NPEER)
    def _(i):
        ship(i)

    @pl.loop(NBM, NB)
    def _(b):
        at = NPEER * MROWS + (b - NBM) * RB
        pool[pl.ds(pl.multiple_of(at, MROWS), RB), :] = physics(b)

    rep = onehot(iota((16, 4), 0) // 4 == iota((16, 4), 1)).astype(BF16)
    fw16 = dot(rep, fw_ref[...]).astype(BF16)
    level = jnp.where(iota((16, NF), 0) == 0, NF // 2 - 1, NF - 1)
    ends = onehot((iota((16, NF), 1) == level) & (iota((16, NF), 0) < 2)).astype(BF16)

    @pl.loop(0, NB)
    def _(b):
        for j in range(EB):
            at = scal_s[1, b * EB + j] * ND
            xs[j * ND : (j + 1) * ND, :] = ordered[pl.ds(at, ND), :]
        tend = xs[...]
        rows = pl.ds(pl.multiple_of(b * RB, RB), RB)
        old = state[rows, :]
        new = (old.astype(F32) + dot(dblk[...], old) + tend.astype(F32)).astype(BF16)
        new_ref[rows, :] = new
        flux16[:, rows] = dot_nt(fw16, tend)
        land[:, rows] = dot_nt(ends, new)

    row_hi = (iota((128, CB), 0) // 16) * 4 + iota((128, CB), 0) % 4
    row_lo = iota((128, CB), 0)
    facc[...] = jnp.zeros((128, 128), F32)

    @pl.loop(0, ROWS // CB)
    def _(c):
        cols = pl.ds(pl.multiple_of(c * CB, CB), CB)
        vals = flux16[:, cols]
        acc = jnp.zeros((128, 128), F32)
        for k in range(4):
            cell = cell_ref[k : k + 1, cols]
            weighted = vals * weight_ref[k : k + 1, cols]
            spread_w = jnp.concatenate([weighted] * 8, axis=0)
            a = jnp.where(row_hi == (cell >> 7), spread_w, 0.0).astype(BF16)
            b = onehot(row_lo == (cell & 127)).astype(BF16)
            acc += dot_nt(a, b)
        facc[...] += acc

    rs_out[...] = facc[...].astype(BF16)

    def rs_copy(q):
        return pltpu.make_async_remote_copy(
            src_ref=rs_out.at[pl.ds(pl.multiple_of(sea(q) * 16, 16), 16)],
            dst_ref=rs_in.at[q],
            send_sem=rsend.at[q],
            recv_sem=rrecv.at[q],
            device_id=(atm, sea(q)),
            device_id_type=MESH,
        )

    def ag_copy(q):
        return pltpu.make_async_remote_copy(
            src_ref=table.at[ocn],
            dst_ref=table.at[ocn],
            send_sem=asend.at[q],
            recv_sem=arecv.at[q],
            device_id=(atm, sea(q)),
            device_id_type=MESH,
        )

    for q in range(1, NOCN):
        rs_copy(q).start()
    share = facc[pl.ds(pl.multiple_of(ocn * 16, 16), 16), :]
    for q in range(1, NOCN):
        rs_copy(q).wait()
        share += rs_in[q].astype(F32)
    sea_mask = omask_ref[...].astype(F32)
    rows_out = []
    for s in range(2):
        forcing = jnp.zeros((4, 128), F32)
        for f in range(4):
            forcing += couple_ref[s, f] * share[f * 4 : (f + 1) * 4, :]
        old = jnp.concatenate(
            [ostate_ref[s : s + 1, h * 128 : (h + 1) * 128] for h in range(4)], axis=0
        )
        new = old + sea_mask * jnp.tanh(forcing)
        for h in range(4):
            onew_ref[s : s + 1, h * 128 : (h + 1) * 128] = new[h : h + 1, :]
        rows_out.append(sea_mask * new)
    table[ocn] = jnp.concatenate(rows_out + [sea_mask, jnp.zeros((4, 128), F32)], axis=0)
    for q in range(1, NOCN):
        ag_copy(q).start()

    def msg_wait(i, places):
        msg_copy(i).wait()
        got = msg_in[i]
        both = jnp.concatenate([got & 255, got >> 8], axis=0)
        return places + jnp.where(both > 0, both + (i * MOVE - 1), 0)

    got = msg_out[NPEER]
    both = jnp.concatenate([got & 255, got >> 8], axis=0)
    places = jnp.where(both > 0, both + (NPEER * MOVE - 1), 0)
    q_v[...] = lax.fori_loop(0, NPEER, msg_wait, places)
    for q in range(1, NOCN):
        ag_copy(q).wait()
    whole = table[...].reshape(128, 128)
    coarse = whole.astype(BF16)
    fine = (whole - coarse.astype(F32)).astype(BF16)
    split = jnp.concatenate([coarse, fine], axis=1)

    @pl.loop(0, ROWS // CB)
    def _(c):
        cols = pl.ds(pl.multiple_of(c * CB, CB), CB)
        acc = jnp.zeros((16, CB), F32)
        for k in range(4):
            cell = cell_ref[k : k + 1, cols]
            b = onehot(row_lo == (cell & 127)).astype(BF16)
            got = dot(split, jnp.concatenate([b, b], axis=0))
            got = jnp.where(row_hi == (cell >> 7), got, 0.0)
            part = got[0:16]
            for o in range(1, 8):
                part += got[o * 16 : (o + 1) * 16]
            acc += part * weight_ref[k : k + 1, cols]
        rest = 1.0 - jnp.sum(acc[8:12], axis=0, keepdims=True)
        ground = land[:, cols]
        for s in range(2):
            sea_part = jnp.sum(acc[s * 4 : (s + 1) * 4], axis=0, keepdims=True)
            surf_ref[s : s + 1, cols] = sea_part + rest * ground[s : s + 1]

    @pl.loop(0, NPEER)
    def _(i):
        data_copy(i).wait()


def place_kernel(q_hbm, pool, new_ref, onew_ref, surf_ref, new_out, tend_out, onew_out, surf_out, stage, q_s, sem):
    copies = [
        pltpu.make_async_copy(src, dst, sem.at[n])
        for n, (src, dst) in enumerate(
            [(q_hbm, q_s), (new_ref, new_out), (onew_ref, onew_out), (surf_ref, surf_out)]
        )
    ]
    for copy in copies:
        copy.start()
    copies[0].wait()

    def part(n):
        rows = pl.ds(pl.multiple_of(n * PLACE * ND, PLACE * ND), PLACE * ND)
        return pltpu.make_async_copy(stage.at[rows], tend_out.at[rows], sem.at[4 + n])

    @pl.loop(0, NE // PLACE)
    def _(n):
        for j in range(PLACE):
            s = n * PLACE + j
            at = pl.multiple_of(q_s[s // 128, lax.rem(s, 128)] * ND, ND)
            stage[pl.ds(pl.multiple_of(s * ND, ND), ND), :] = pool[pl.ds(at, ND), :]
        part(n).start()

    for copy in copies[1:]:
        copy.wait()

    @pl.loop(0, NE // PLACE)
    def _(n):
        part(n).wait()


def body(
    state,
    branch_id,
    span_map,
    derivative,
    rad_weight,
    conv_in,
    conv_out,
    flux_weight,
    remap_cell,
    remap_weight,
    ocean_state,
    ocean_mask,
    couple,
):
    vmem = pl.BlockSpec(memory_space=pltpu.VMEM)
    hbm = pl.BlockSpec(memory_space=pltpu.HBM)
    dma = pltpu.SemaphoreType.DMA
    in_hbm = lambda a: pltpu.with_memory_space_constraint(a, pltpu.HBM)
    stay = lambda a: pltpu.with_memory_space_constraint(a, pltpu.VMEM)
    in_vmem = pltpu.VMEM
    out_hbm = pltpu.HBM
    plan = pl.pallas_call(
        plan_kernel,
        out_shape=(
            in_vmem((8, NE), I32),
            in_vmem((32, 1, 128), I32),
            in_vmem((NE, 128), BF16),
            in_vmem((RB, RB), BF16),
        ),
        in_specs=[hbm] * 3,
        out_specs=(vmem,) * 4,
        scratch_shapes=[
            pltpu.VMEM((1, NE), I32),
            pltpu.VMEM((32, 128), I32),
            pltpu.VMEM((ND, ND), BF16),
            dma((3,)),
        ],
        compiler_params=pltpu.CompilerParams(vmem_limit_bytes=8 << 20),
    )(in_hbm(span_map.reshape(1, NE)), in_hbm(branch_id.reshape(32, 128)), in_hbm(derivative))
    new_state, pool, places, ocean_new, surface = pl.pallas_call(
        kernel,
        out_shape=(
            in_vmem((ROWS, NF), BF16),
            in_vmem((NPEER * MROWS + NMOVED * ND, NF), BF16),
            in_vmem((2, 128), I32),
            in_vmem((2, 512), F32),
            in_vmem((2, ROWS), F32),
        ),
        in_specs=[vmem] * 4 + [hbm] * 10,
        out_specs=(vmem,) * 5,
        scratch_shapes=[
            pltpu.VMEM((ROWS, NF), BF16),
            pltpu.VMEM((NF, 2048), BF16),
            pltpu.VMEM((NF, 2048), BF16),
            pltpu.VMEM((2048, NF), BF16),
            pltpu.VMEM((4, NF), BF16),
            pltpu.VMEM((4, ROWS), I32),
            pltpu.VMEM((4, ROWS), F32),
            pltpu.VMEM((2, 512), F32),
            pltpu.VMEM((4, 128), I32),
            pltpu.SMEM((2, 4), F32),
            pltpu.VMEM((RB, NF), BF16),
            pltpu.VMEM((ROWS, NF), BF16),
            pltpu.VMEM((NPEER, MROWS, NF), BF16),
            pltpu.VMEM((32, 1, 128), I32),
            pltpu.SMEM((8, NE), I32),
            pltpu.VMEM((16, ROWS), F32),
            pltpu.VMEM((16, ROWS), F32),
            pltpu.VMEM((128, 128), F32),
            pltpu.VMEM((128, 128), BF16),
            pltpu.VMEM((NOCN, 16, 128), BF16),
            pltpu.VMEM((NOCN, 16, 128), F32),
            dma((11,)),
            dma((NPEER,)),
            dma((NPEER,)),
            dma((NPEER,)),
            dma((NPEER,)),
            dma((NOCN,)),
            dma((NOCN,)),
            dma((NOCN,)),
            dma((NOCN,)),
        ],
        compiler_params=pltpu.CompilerParams(
            collective_id=0, has_side_effects=True, vmem_limit_bytes=32 << 20
        ),
        cost_estimate=pl.CostEstimate(
            flops=14_000_000_000, bytes_accessed=12_000_000, transcendentals=17_000_000
        ),
    )(
        *plan,
        *(
            in_hbm(a)
            for a in (
                couple.T,
                flux_weight.T,
                remap_cell,
                remap_weight,
                ocean_state,
                ocean_mask.reshape(4, 128),
                state,
                rad_weight,
                conv_in,
                conv_out,
            )
        ),
    )
    new_state, span_tend, ocean_new, surface = pl.pallas_call(
        place_kernel,
        out_shape=(
            out_hbm((ROWS, NF), BF16),
            out_hbm((ROWS, NF), BF16),
            out_hbm((2, 512), F32),
            out_hbm((2, ROWS), F32),
        ),
        in_specs=[vmem] * 5,
        out_specs=(hbm,) * 4,
        scratch_shapes=[
            pltpu.VMEM((ROWS, NF), BF16),
            pltpu.SMEM((2, 128), I32),
            dma((4 + NE // PLACE,)),
        ],
        compiler_params=pltpu.CompilerParams(vmem_limit_bytes=8 << 20),
    )(*(stay(a) for a in (places, pool, new_state, ocean_new, surface)))
    return new_state, span_tend, ocean_new, surface


def solution(mesh):
    cols = P(("atm", "ocn"), None)
    flat = P(("atm", "ocn"))
    lanes = P(None, ("atm", "ocn"))
    return jax.shard_map(
        body,
        mesh=mesh,
        in_specs=(cols, flat, flat, P(), P(), P(), P(), P(), lanes, lanes, lanes, flat, P()),
        out_specs=(cols, cols, lanes, lanes),
        check_vma=False,
    )
```

```python
import jax
import jax.numpy as jnp
from jax import lax
from jax.experimental import pallas as pl
from jax.experimental.pallas import tpu as pltpu
from jax.sharding import PartitionSpec as P

MESH = pl.DeviceIdType.MESH
F32 = jnp.float32
BF16 = jnp.bfloat16
I32 = jnp.int32

NX, NZ = 4, 8
NPEER = NX * NZ - 1
NOCN = 8
NY = 4
NE = 256
ND = 16
NF = 256
ROWS = NE * ND
MOVE = 8
MROWS = MOVE * ND
NMOVED = NE // 2
RB = 256
EB = RB // ND
NB = ROWS // RB
NBM = NMOVED // EB
CB = 512
PLACE = 16


def iota(shape, dim):
    return lax.broadcasted_iota(I32, shape, dim)


def onehot(cond):
    return jnp.where(cond, 1.0, 0.0).astype(F32)


def dot(a, b):
    return jnp.dot(a, b, preferred_element_type=F32)


def dot_nt(a, b):
    return lax.dot_general(a, b, (((1,), (1,)), ((), ())), preferred_element_type=F32)


def column(row):
    parts = [
        jnp.broadcast_to(row[:, h * 128 : (h + 1) * 128], (128, 128)).T for h in range(2)
    ]
    half = jnp.concatenate(parts, axis=0)
    return jnp.concatenate([half, half], axis=1)


def kernel(
    span_hbm,
    branch_hbm,
    deriv_hbm,
    couple_hbm,
    fw_hbm,
    cell_hbm,
    weight_hbm,
    ostate_hbm,
    omask_hbm,
    state_hbm,
    rad_hbm,
    cin_hbm,
    cout_hbm,
    new_ref,
    pool,
    q_v,
    onew_ref,
    surf_ref,
    span_ref,
    branch_ref,
    deriv_ref,
    couple_ref,
    fw_ref,
    cell_ref,
    weight_ref,
    ostate_ref,
    omask_ref,
    state,
    rad,
    cin,
    cout,
    ordered,
    mask_ord,
    send,
    msg_out,
    msg_in,
    scal_v,
    scal_s,
    dblk,
    flux16,
    land,
    facc,
    rs_out,
    rs_in,
    table,
    second,
    load_sem,
    dsend,
    drecv,
    msend,
    mrecv,
    rsend,
    rrecv,
    asend,
    arecv,
):
    atm = lax.axis_index("atm")
    ocn = lax.axis_index("ocn")
    x = atm // NZ
    z = lax.rem(atm, NZ)
    y = ocn // 2
    core = lax.rem(ocn, 2)

    def at_offset(dx, dz):
        return lax.rem(x + dx, NX) * NZ + lax.rem(z + dz, NZ)

    def peer(i):
        rel = i + 1
        return at_offset(rel // NZ, lax.rem(rel, NZ))

    def sea(q):
        return lax.rem(ocn + q, NOCN)

    barrier = pltpu.get_barrier_semaphore()
    along_x = [at_offset(dx, 0) for dx in range(1, NX)]
    along_z = [at_offset(0, dz) for dz in range(1, NZ)]
    along_y = [lax.rem(y + dy, NY) * 2 + core for dy in range(1, NY)]
    mate = y * 2 + 1 - core
    for to in along_z + along_x:
        pl.semaphore_signal(barrier, inc=1, device_id=(to, ocn), device_id_type=MESH)
    for to in along_y + [mate]:
        pl.semaphore_signal(barrier, inc=1, device_id=(atm, to), device_id_type=MESH)
    first_count = len(along_x) + len(along_z) + len(along_y) + 1

    small = [(span_hbm, span_ref), (branch_hbm, branch_ref), (deriv_hbm, deriv_ref)]
    large = [
        (state_hbm, state),
        (rad_hbm, rad),
        (cin_hbm, cin),
        (cout_hbm, cout),
        (fw_hbm, fw_ref),
        (cell_hbm, cell_ref),
        (weight_hbm, weight_ref),
        (ostate_hbm, ostate_ref),
        (omask_hbm, omask_ref),
        (couple_hbm, couple_ref),
    ]
    loads = [
        pltpu.make_async_copy(src, dst, load_sem.at[n])
        for n, (src, dst) in enumerate(small + large)
    ]
    for copy in loads:
        copy.start()
    for copy in loads[: len(small)]:
        copy.wait()

    span = span_ref[...]
    target = span >> 11
    rel = ((((target >> 3) - x) & (NX - 1)) << 3) + (((target & (NZ - 1)) - z) & (NZ - 1))
    key_r = jnp.where(rel == 0, NPEER, rel - 1)
    both_r = key_r * NE + iota((1, NE), 1)
    key_c = column(key_r)
    both_c = column(both_r)
    lane = iota((NE, NE), 1)
    sub = iota((NE, NE), 0)

    def count(cond):
        return jnp.sum(jnp.where(cond, 1, 0), axis=0, keepdims=True)

    pos_r = count(both_c < both_r)
    src_r = jnp.sum(jnp.where(column(pos_r) == lane, sub, 0), axis=0, keepdims=True)
    scal_v[0:1, :] = src_r
    scal_v[1:2, :] = pos_r
    scal_v[2:3, :] = jnp.minimum(count(key_c < lane), NMOVED)
    scal_copy = pltpu.make_async_copy(scal_v, scal_s, load_sem.at[len(loads)])
    scal_copy.start()
    rank_r = jnp.where(key_r == NPEER, pos_r - (NMOVED - 1), pos_r - count(key_c < key_r) + 1)
    pick = jnp.where(key_r == iota((32, NE), 0), rank_r, 0).astype(F32).astype(BF16)
    slots = onehot(column(span & (NE - 1)) == lane).astype(BF16)
    msg = dot(pick, slots)
    packed = (msg[:, :128] + 256.0 * msg[:, 128:]).astype(I32)
    for i in range(32):
        msg_out[i] = packed[i : i + 1, :]
    bits = branch_ref[...].astype(F32).astype(BF16)
    spread = dot(onehot(iota((NE, 32), 0) // 8 == iota((NE, 32), 1)).astype(BF16), bits)
    own = jnp.where(iota((NE, 128), 1) // ND == iota((NE, 128), 0) % 8, spread, 0.0)
    fold = onehot(iota((128, 128), 0) % ND == iota((128, 128), 1) % ND).astype(BF16)
    bits_nat = dot(own.astype(BF16), fold).astype(BF16)
    order = onehot(pos_r == sub).astype(BF16)
    mask_ord[...] = dot(order, bits_nat).astype(BF16)
    spread_rows = onehot(iota((RB, ND), 0) % ND == iota((RB, ND), 1)).astype(BF16)
    tiled = dot_nt(dot(spread_rows, deriv_ref[...]).astype(BF16), spread_rows)
    same = iota((RB, RB), 0) // ND == iota((RB, RB), 1) // ND
    dblk[...] = jnp.where(same, tiled, 0.0).astype(BF16)
    for copy in loads[len(small) :]:
        copy.wait()
    scal_copy.wait()

    to_rows = onehot(iota((RB, EB), 0) // ND == iota((RB, EB), 1)).astype(BF16)
    my_lane = iota((RB, 128), 1) == iota((RB, 128), 0) % ND
    ones = jnp.ones((128, NF), BF16)

    def gather(ref, row, b):
        rows = [ref[pl.ds(scal_s[row, b * EB + j] * ND, ND), :] for j in range(EB)]
        return jnp.concatenate(rows, axis=0)

    def physics(b):
        cols = gather(state, 0, b)
        total = jnp.zeros((RB, NF), F32)
        conv = jnp.zeros((RB, NF), F32)
        for g in range(8):
            part = slice(g * NF, (g + 1) * NF)
            total += jnp.tanh(dot(cols, rad[:, part]))
            half = 0.5 * dot(cols, cin[:, part])
            hidden = (half * (1.0 + jnp.tanh(half))).astype(BF16)
            conv += dot(hidden, cout[part, :])
        bits_b = mask_ord[pl.ds(pl.multiple_of(b * EB, EB), EB), :]
        mine = jnp.where(my_lane, dot(to_rows, bits_b), 0.0).astype(BF16)
        mask = dot(mine, ones)
        out = (0.25 * total + mask * conv).astype(BF16)
        ordered[pl.ds(pl.multiple_of(b * RB, RB), RB), :] = out

    def data_copy(i):
        return pltpu.make_async_remote_copy(
            src_ref=send.at[i],
            dst_ref=pool.at[pl.ds(pl.multiple_of(i * MROWS, MROWS), MROWS)],
            send_sem=dsend.at[i],
            recv_sem=drecv.at[i],
            device_id=(peer(i), ocn),
            device_id_type=MESH,
        )

    def msg_copy(i):
        return pltpu.make_async_remote_copy(
            src_ref=msg_out.at[i],
            dst_ref=msg_in.at[i],
            send_sem=msend.at[i],
            recv_sem=mrecv.at[i],
            device_id=(peer(i), ocn),
            device_id_type=MESH,
        )

    def ship(i):
        at = scal_s[2, i] * ND
        send[i] = ordered[pl.ds(at, MROWS), :]
        data_copy(i).start()

    per_block = EB // MOVE

    @pl.loop(0, NB)
    def _(b):
        physics(b)

        @pl.when(b == 0)
        def _():
            pl.semaphore_wait(barrier, first_count)
            for to in along_x:
                pl.semaphore_signal(second, inc=1, device_id=(to, ocn), device_id_type=MESH)
            pl.semaphore_signal(second, inc=1, device_id=(atm, mate), device_id_type=MESH)

        @pl.when(b == 3)
        def _():
            pl.semaphore_wait(second, len(along_x) + 1)

            @pl.loop(0, NPEER)
            def _(i):
                msg_copy(i).start()

        @pl.when(b < NBM)
        def _():
            for i in range(per_block):
                ship(b * per_block + i)

        @pl.when(b == NBM - 1)
        def _():
            @pl.loop(NBM * per_block, NPEER)
            def _(i):
                ship(i)

    @pl.loop(0, NB - NBM)
    def _(n):
        at = pl.ds(pl.multiple_of(NPEER * MROWS + n * RB, MROWS), RB)
        pool[at, :] = ordered[pl.ds(pl.multiple_of((NBM + n) * RB, RB), RB), :]

    rep = onehot(iota((16, 4), 0) // 4 == iota((16, 4), 1)).astype(BF16)
    fw16 = dot(rep, fw_ref[...]).astype(BF16)
    level = jnp.where(iota((16, NF), 0) == 0, NF // 2 - 1, NF - 1)
    ends = onehot((iota((16, NF), 1) == level) & (iota((16, NF), 0) < 2)).astype(BF16)

    @pl.loop(0, NB)
    def _(b):
        tend = gather(ordered, 1, b)
        rows = pl.ds(pl.multiple_of(b * RB, RB), RB)
        old = state[rows, :]
        new = (old.astype(F32) + dot(dblk[...], old) + tend.astype(F32)).astype(BF16)
        new_ref[rows, :] = new
        flux16[:, rows] = dot_nt(fw16, tend)
        land[:, rows] = dot_nt(ends, new)

    row_hi = (iota((128, CB), 0) // 16) * 4 + iota((128, CB), 0) % 4
    row_lo = iota((128, CB), 0)
    facc[...] = jnp.zeros((128, 128), F32)

    @pl.loop(0, ROWS // CB)
    def _(c):
        cols = pl.ds(pl.multiple_of(c * CB, CB), CB)
        vals = flux16[:, cols]
        acc = jnp.zeros((128, 128), F32)
        for k in range(4):
            cell = cell_ref[k : k + 1, cols]
            weighted = vals * weight_ref[k : k + 1, cols]
            spread_w = jnp.concatenate([weighted] * 8, axis=0)
            a = jnp.where(row_hi == (cell >> 7), spread_w, 0.0).astype(BF16)
            b = onehot(row_lo == (cell & 127)).astype(BF16)
            acc += dot_nt(a, b)
        facc[...] += acc

    rs_out[...] = facc[...].astype(BF16)

    def rs_copy(q):
        return pltpu.make_async_remote_copy(
            src_ref=rs_out.at[pl.ds(pl.multiple_of(sea(q) * 16, 16), 16)],
            dst_ref=rs_in.at[q],
            send_sem=rsend.at[q],
            recv_sem=rrecv.at[q],
            device_id=(atm, sea(q)),
            device_id_type=MESH,
        )

    def ag_copy(q):
        return pltpu.make_async_remote_copy(
            src_ref=table.at[ocn],
            dst_ref=table.at[ocn],
            send_sem=asend.at[q],
            recv_sem=arecv.at[q],
            device_id=(atm, sea(q)),
            device_id_type=MESH,
        )

    for q in range(1, NOCN):
        rs_copy(q).start()
    share = facc[pl.ds(pl.multiple_of(ocn * 16, 16), 16), :]
    for q in range(1, NOCN):
        rs_copy(q).wait()
        share += rs_in[q].astype(F32)
    sea_mask = omask_ref[...].astype(F32)
    rows_out = []
    for s in range(2):
        forcing = jnp.zeros((4, 128), F32)
        for f in range(4):
            forcing += couple_ref[s, f] * share[f * 4 : (f + 1) * 4, :]
        old = jnp.concatenate(
            [ostate_ref[s : s + 1, h * 128 : (h + 1) * 128] for h in range(4)], axis=0
        )
        new = old + sea_mask * jnp.tanh(forcing)
        for h in range(4):
            onew_ref[s : s + 1, h * 128 : (h + 1) * 128] = new[h : h + 1, :]
        rows_out.append(sea_mask * new)
    table[ocn] = jnp.concatenate(rows_out + [sea_mask, jnp.zeros((4, 128), F32)], axis=0)
    for q in range(1, NOCN):
        ag_copy(q).start()

    def msg_wait(i, places):
        msg_copy(i).wait()
        got = msg_in[i]
        both = jnp.concatenate([got & 255, got >> 8], axis=0)
        return places + jnp.where(both > 0, both + (i * MOVE - 1), 0)

    got = msg_out[NPEER]
    both = jnp.concatenate([got & 255, got >> 8], axis=0)
    places = jnp.where(both > 0, both + (NPEER * MOVE - 1), 0)
    q_v[...] = lax.fori_loop(0, NPEER, msg_wait, places)
    for q in range(1, NOCN):
        ag_copy(q).wait()
    whole = table[...].reshape(128, 128)
    coarse = whole.astype(BF16)
    fine = (whole - coarse.astype(F32)).astype(BF16)
    split = jnp.concatenate([coarse, fine], axis=1)

    @pl.loop(0, ROWS // CB)
    def _(c):
        cols = pl.ds(pl.multiple_of(c * CB, CB), CB)
        acc = jnp.zeros((16, CB), F32)
        for k in range(4):
            cell = cell_ref[k : k + 1, cols]
            b = onehot(row_lo == (cell & 127)).astype(BF16)
            got = dot(split, jnp.concatenate([b, b], axis=0))
            got = jnp.where(row_hi == (cell >> 7), got, 0.0)
            part = got[0:16]
            for o in range(1, 8):
                part += got[o * 16 : (o + 1) * 16]
            acc += part * weight_ref[k : k + 1, cols]
        rest = 1.0 - jnp.sum(acc[8:12], axis=0, keepdims=True)
        ground = land[:, cols]
        for s in range(2):
            sea_part = jnp.sum(acc[s * 4 : (s + 1) * 4], axis=0, keepdims=True)
            surf_ref[s : s + 1, cols] = sea_part + rest * ground[s : s + 1]

    @pl.loop(0, NPEER)
    def _(i):
        data_copy(i).wait()


def place_kernel(q_hbm, pool, new_ref, onew_ref, surf_ref, new_out, tend_out, onew_out, surf_out, stage, q_s, sem):
    copies = [
        pltpu.make_async_copy(src, dst, sem.at[n])
        for n, (src, dst) in enumerate(
            [(q_hbm, q_s), (new_ref, new_out), (onew_ref, onew_out), (surf_ref, surf_out)]
        )
    ]
    for copy in copies:
        copy.start()
    copies[0].wait()

    def part(n):
        rows = pl.ds(pl.multiple_of(n * PLACE * ND, PLACE * ND), PLACE * ND)
        return pltpu.make_async_copy(stage.at[rows], tend_out.at[rows], sem.at[4 + n])

    @pl.loop(0, NE // PLACE)
    def _(n):
        rows = []
        for j in range(PLACE):
            s = n * PLACE + j
            at = pl.multiple_of(q_s[s // 128, lax.rem(s, 128)] * ND, ND)
            rows.append(pool[pl.ds(at, ND), :])
        block = pl.ds(pl.multiple_of(n * PLACE * ND, PLACE * ND), PLACE * ND)
        stage[block, :] = jnp.concatenate(rows, axis=0)
        part(n).start()

    for copy in copies[1:]:
        copy.wait()

    @pl.loop(0, NE // PLACE)
    def _(n):
        part(n).wait()


def body(
    state,
    branch_id,
    span_map,
    derivative,
    rad_weight,
    conv_in,
    conv_out,
    flux_weight,
    remap_cell,
    remap_weight,
    ocean_state,
    ocean_mask,
    couple,
):
    vmem = pl.BlockSpec(memory_space=pltpu.VMEM)
    hbm = pl.BlockSpec(memory_space=pltpu.HBM)
    dma = pltpu.SemaphoreType.DMA
    in_hbm = lambda a: pltpu.with_memory_space_constraint(a, pltpu.HBM)
    stay = lambda a: pltpu.with_memory_space_constraint(a, pltpu.VMEM)
    in_vmem = pltpu.VMEM
    out_hbm = pltpu.HBM
    new_state, pool, places, ocean_new, surface = pl.pallas_call(
        kernel,
        out_shape=(
            in_vmem((ROWS, NF), BF16),
            in_vmem((NPEER * MROWS + NMOVED * ND, NF), BF16),
            in_vmem((2, 128), I32),
            in_vmem((2, 512), F32),
            in_vmem((2, ROWS), F32),
        ),
        in_specs=[hbm] * 13,
        out_specs=(vmem,) * 5,
        scratch_shapes=[
            pltpu.VMEM((1, NE), I32),
            pltpu.VMEM((32, 128), I32),
            pltpu.VMEM((ND, ND), BF16),
            pltpu.SMEM((2, 4), F32),
            pltpu.VMEM((4, NF), BF16),
            pltpu.VMEM((4, ROWS), I32),
            pltpu.VMEM((4, ROWS), F32),
            pltpu.VMEM((2, 512), F32),
            pltpu.VMEM((4, 128), I32),
            pltpu.VMEM((ROWS, NF), BF16),
            pltpu.VMEM((NF, 2048), BF16),
            pltpu.VMEM((NF, 2048), BF16),
            pltpu.VMEM((2048, NF), BF16),
            pltpu.VMEM((ROWS, NF), BF16),
            pltpu.VMEM((NE, 128), BF16),
            pltpu.VMEM((NPEER, MROWS, NF), BF16),
            pltpu.VMEM((32, 1, 128), I32),
            pltpu.VMEM((32, 1, 128), I32),
            pltpu.VMEM((8, NE), I32),
            pltpu.SMEM((8, NE), I32),
            pltpu.VMEM((RB, RB), BF16),
            pltpu.VMEM((16, ROWS), F32),
            pltpu.VMEM((16, ROWS), F32),
            pltpu.VMEM((128, 128), F32),
            pltpu.VMEM((128, 128), BF16),
            pltpu.VMEM((NOCN, 16, 128), BF16),
            pltpu.VMEM((NOCN, 16, 128), F32),
            pltpu.SemaphoreType.REGULAR,
            dma((14,)),
            dma((NPEER,)),
            dma((NPEER,)),
            dma((NPEER,)),
            dma((NPEER,)),
            dma((NOCN,)),
            dma((NOCN,)),
            dma((NOCN,)),
            dma((NOCN,)),
        ],
        compiler_params=pltpu.CompilerParams(
            collective_id=0, has_side_effects=True, vmem_limit_bytes=32 << 20
        ),
        cost_estimate=pl.CostEstimate(
            flops=14_000_000_000, bytes_accessed=12_000_000, transcendentals=17_000_000
        ),
    )(
        *(
            in_hbm(a)
            for a in (
                span_map.reshape(1, NE),
                branch_id.reshape(32, 128),
                derivative,
                couple.T,
                flux_weight.T,
                remap_cell,
                remap_weight,
                ocean_state,
                ocean_mask.reshape(4, 128),
                state,
                rad_weight,
                conv_in,
                conv_out,
            )
        ),
    )
    new_state, span_tend, ocean_new, surface = pl.pallas_call(
        place_kernel,
        out_shape=(
            out_hbm((ROWS, NF), BF16),
            out_hbm((ROWS, NF), BF16),
            out_hbm((2, 512), F32),
            out_hbm((2, ROWS), F32),
        ),
        in_specs=[vmem] * 5,
        out_specs=(hbm,) * 4,
        scratch_shapes=[
            pltpu.VMEM((ROWS, NF), BF16),
            pltpu.SMEM((2, 128), I32),
            dma((4 + NE // PLACE,)),
        ],
        compiler_params=pltpu.CompilerParams(vmem_limit_bytes=8 << 20),
    )(*(stay(a) for a in (places, pool, new_state, ocean_new, surface)))
    return new_state, span_tend, ocean_new, surface


def solution(mesh):
    cols = P(("atm", "ocn"), None)
    flat = P(("atm", "ocn"))
    lanes = P(None, ("atm", "ocn"))
    return jax.shard_map(
        body,
        mesh=mesh,
        in_specs=(cols, flat, flat, P(), P(), P(), P(), P(), lanes, lanes, lanes, flat, P()),
        out_specs=(cols, cols, lanes, lanes),
        check_vma=False,
    )
```

```python
import jax
import jax.numpy as jnp
from jax import lax
from jax.experimental import pallas as pl
from jax.experimental.pallas import tpu as pltpu
from jax.sharding import PartitionSpec as P

MESH = pl.DeviceIdType.MESH
F32 = jnp.float32
BF16 = jnp.bfloat16
I32 = jnp.int32

NX, NZ = 4, 8
NPEER = NX * NZ - 1
NOCN = 8
NY = 4
NE = 256
ND = 16
NF = 256
ROWS = NE * ND
MOVE = 8
MROWS = MOVE * ND
NMOVED = NE // 2
RB = 256
EB = RB // ND
NB = ROWS // RB
NBM = NMOVED // EB
CB = 512
PLACE = 16


def iota(shape, dim):
    return lax.broadcasted_iota(I32, shape, dim)


def onehot(cond):
    return jnp.where(cond, 1.0, 0.0).astype(F32)


def dot(a, b):
    return jnp.dot(a, b, preferred_element_type=F32)


def dot_nt(a, b):
    return lax.dot_general(a, b, (((1,), (1,)), ((), ())), preferred_element_type=F32)


def column(row):
    parts = [
        jnp.broadcast_to(row[:, h * 128 : (h + 1) * 128], (128, 128)).T for h in range(2)
    ]
    half = jnp.concatenate(parts, axis=0)
    return jnp.concatenate([half, half], axis=1)


def kernel(
    span_hbm,
    branch_hbm,
    deriv_hbm,
    couple_hbm,
    fw_hbm,
    cell_hbm,
    weight_hbm,
    ostate_hbm,
    omask_hbm,
    state_hbm,
    rad_hbm,
    cin_hbm,
    cout_hbm,
    new_ref,
    pool,
    q_s,
    onew_ref,
    surf_ref,
    span_ref,
    branch_ref,
    deriv_ref,
    couple_ref,
    fw_ref,
    cell_ref,
    weight_ref,
    ostate_ref,
    omask_ref,
    state,
    rad,
    cin,
    cout,
    ordered,
    mask_ord,
    send,
    msg_out,
    msg_in,
    scal_v,
    scal_s,
    dblk,
    flux16,
    land,
    facc,
    rs_out,
    rs_in,
    table,
    second,
    q_v,
    load_sem,
    dsend,
    drecv,
    msend,
    mrecv,
    rsend,
    rrecv,
    asend,
    arecv,
):
    atm = lax.axis_index("atm")
    ocn = lax.axis_index("ocn")
    x = atm // NZ
    z = lax.rem(atm, NZ)
    y = ocn // 2
    core = lax.rem(ocn, 2)

    def at_offset(dx, dz):
        return lax.rem(x + dx, NX) * NZ + lax.rem(z + dz, NZ)

    def peer(i):
        rel = i + 1
        return at_offset(rel // NZ, lax.rem(rel, NZ))

    def sea(q):
        return lax.rem(ocn + q, NOCN)

    barrier = pltpu.get_barrier_semaphore()
    along_x = [at_offset(dx, 0) for dx in range(1, NX)]
    along_z = [at_offset(0, dz) for dz in range(1, NZ)]
    along_y = [lax.rem(y + dy, NY) * 2 + core for dy in range(1, NY)]
    mate = y * 2 + 1 - core
    for to in along_z + along_x:
        pl.semaphore_signal(barrier, inc=1, device_id=(to, ocn), device_id_type=MESH)
    for to in along_y + [mate]:
        pl.semaphore_signal(barrier, inc=1, device_id=(atm, to), device_id_type=MESH)
    first_count = len(along_x) + len(along_z) + len(along_y) + 1

    small = [(span_hbm, span_ref), (branch_hbm, branch_ref), (deriv_hbm, deriv_ref)]
    large = [
        (state_hbm, state),
        (rad_hbm, rad),
        (cin_hbm, cin),
        (cout_hbm, cout),
        (fw_hbm, fw_ref),
        (cell_hbm, cell_ref),
        (weight_hbm, weight_ref),
        (ostate_hbm, ostate_ref),
        (omask_hbm, omask_ref),
        (couple_hbm, couple_ref),
    ]
    loads = [
        pltpu.make_async_copy(src, dst, load_sem.at[n])
        for n, (src, dst) in enumerate(small + large)
    ]
    for copy in loads:
        copy.start()
    for copy in loads[: len(small)]:
        copy.wait()

    span = span_ref[...]
    target = span >> 11
    rel = ((((target >> 3) - x) & (NX - 1)) << 3) + (((target & (NZ - 1)) - z) & (NZ - 1))
    key_r = jnp.where(rel == 0, NPEER, rel - 1)
    both_r = key_r * NE + iota((1, NE), 1)
    key_c = column(key_r)
    both_c = column(both_r)
    lane = iota((NE, NE), 1)
    sub = iota((NE, NE), 0)

    def count(cond):
        return jnp.sum(jnp.where(cond, 1, 0), axis=0, keepdims=True)

    pos_r = count(both_c < both_r)
    src_r = jnp.sum(jnp.where(column(pos_r) == lane, sub, 0), axis=0, keepdims=True)
    scal_v[0:1, :] = src_r
    scal_v[1:2, :] = pos_r
    scal_v[2:3, :] = jnp.minimum(count(key_c < lane), NMOVED)
    scal_copy = pltpu.make_async_copy(scal_v, scal_s, load_sem.at[len(loads)])
    scal_copy.start()
    rank_r = jnp.where(key_r == NPEER, pos_r - (NMOVED - 1), pos_r - count(key_c < key_r) + 1)
    pick = jnp.where(key_r == iota((32, NE), 0), rank_r, 0).astype(F32).astype(BF16)
    slots = onehot(column(span & (NE - 1)) == lane).astype(BF16)
    msg = dot(pick, slots)
    packed = (msg[:, :128] + 256.0 * msg[:, 128:]).astype(I32)
    for i in range(32):
        msg_out[i] = packed[i : i + 1, :]
    bits = branch_ref[...].astype(F32).astype(BF16)
    spread = dot(onehot(iota((NE, 32), 0) // 8 == iota((NE, 32), 1)).astype(BF16), bits)
    own = jnp.where(iota((NE, 128), 1) // ND == iota((NE, 128), 0) % 8, spread, 0.0)
    fold = onehot(iota((128, 128), 0) % ND == iota((128, 128), 1) % ND).astype(BF16)
    bits_nat = dot(own.astype(BF16), fold).astype(BF16)
    order = onehot(pos_r == sub).astype(BF16)
    mask_ord[...] = dot(order, bits_nat).astype(BF16)
    spread_rows = onehot(iota((RB, ND), 0) % ND == iota((RB, ND), 1)).astype(BF16)
    tiled = dot_nt(dot(spread_rows, deriv_ref[...]).astype(BF16), spread_rows)
    same = iota((RB, RB), 0) // ND == iota((RB, RB), 1) // ND
    dblk[...] = jnp.where(same, tiled, 0.0).astype(BF16)
    for copy in loads[len(small) :]:
        copy.wait()
    scal_copy.wait()

    to_rows = onehot(iota((RB, EB), 0) // ND == iota((RB, EB), 1)).astype(BF16)
    my_lane = iota((RB, 128), 1) == iota((RB, 128), 0) % ND
    ones = jnp.ones((128, NF), BF16)

    def gather(ref, row, b):
        rows = [ref[pl.ds(scal_s[row, b * EB + j] * ND, ND), :] for j in range(EB)]
        return jnp.concatenate(rows, axis=0)

    def physics(b):
        cols = gather(state, 0, b)
        total = jnp.zeros((RB, NF), F32)
        conv = jnp.zeros((RB, NF), F32)
        for g in range(8):
            part = slice(g * NF, (g + 1) * NF)
            total += jnp.tanh(dot(cols, rad[:, part]))
            half = 0.5 * dot(cols, cin[:, part])
            hidden = (half * (1.0 + jnp.tanh(half))).astype(BF16)
            conv += dot(hidden, cout[part, :])
        bits_b = mask_ord[pl.ds(pl.multiple_of(b * EB, EB), EB), :]
        mine = jnp.where(my_lane, dot(to_rows, bits_b), 0.0).astype(BF16)
        mask = dot(mine, ones)
        out = (0.25 * total + mask * conv).astype(BF16)
        ordered[pl.ds(pl.multiple_of(b * RB, RB), RB), :] = out

    def data_copy(i):
        return pltpu.make_async_remote_copy(
            src_ref=send.at[i],
            dst_ref=pool.at[pl.ds(pl.multiple_of(i * MROWS, MROWS), MROWS)],
            send_sem=dsend.at[i],
            recv_sem=drecv.at[i],
            device_id=(peer(i), ocn),
            device_id_type=MESH,
        )

    def msg_copy(i):
        return pltpu.make_async_remote_copy(
            src_ref=msg_out.at[i],
            dst_ref=msg_in.at[i],
            send_sem=msend.at[i],
            recv_sem=mrecv.at[i],
            device_id=(peer(i), ocn),
            device_id_type=MESH,
        )

    def ship(i):
        at = scal_s[2, i] * ND
        send[i] = ordered[pl.ds(at, MROWS), :]
        data_copy(i).start()

    per_block = EB // MOVE

    @pl.loop(0, NB)
    def _(b):
        physics(b)

        @pl.when(b == 0)
        def _():
            pl.semaphore_wait(barrier, first_count)
            for to in along_x:
                pl.semaphore_signal(second, inc=1, device_id=(to, ocn), device_id_type=MESH)
            pl.semaphore_signal(second, inc=1, device_id=(atm, mate), device_id_type=MESH)

        @pl.when(b == 3)
        def _():
            pl.semaphore_wait(second, len(along_x) + 1)

            @pl.loop(0, NPEER)
            def _(i):
                msg_copy(i).start()

        @pl.when(b < NBM)
        def _():
            for i in range(per_block):
                ship(b * per_block + i)

        @pl.when(b == NBM - 1)
        def _():
            @pl.loop(NBM * per_block, NPEER)
            def _(i):
                ship(i)

    @pl.loop(0, NB - NBM)
    def _(n):
        at = pl.ds(pl.multiple_of(NPEER * MROWS + n * RB, MROWS), RB)
        pool[at, :] = ordered[pl.ds(pl.multiple_of((NBM + n) * RB, RB), RB), :]

    rep = onehot(iota((16, 4), 0) // 4 == iota((16, 4), 1)).astype(BF16)
    fw16 = dot(rep, fw_ref[...]).astype(BF16)
    level = jnp.where(iota((16, NF), 0) == 0, NF // 2 - 1, NF - 1)
    ends = onehot((iota((16, NF), 1) == level) & (iota((16, NF), 0) < 2)).astype(BF16)

    @pl.loop(0, NB)
    def _(b):
        tend = gather(ordered, 1, b)
        rows = pl.ds(pl.multiple_of(b * RB, RB), RB)
        old = state[rows, :]
        new = (old.astype(F32) + dot(dblk[...], old) + tend.astype(F32)).astype(BF16)
        new_ref[rows, :] = new
        flux16[:, rows] = dot_nt(fw16, tend)
        land[:, rows] = dot_nt(ends, new)

    row_hi = (iota((128, CB), 0) // 16) * 4 + iota((128, CB), 0) % 4
    row_lo = iota((128, CB), 0)
    facc[...] = jnp.zeros((128, 128), F32)

    @pl.loop(0, ROWS // CB)
    def _(c):
        cols = pl.ds(pl.multiple_of(c * CB, CB), CB)
        vals = flux16[:, cols]
        acc = jnp.zeros((128, 128), F32)
        for k in range(4):
            cell = cell_ref[k : k + 1, cols]
            weighted = vals * weight_ref[k : k + 1, cols]
            spread_w = jnp.concatenate([weighted] * 8, axis=0)
            a = jnp.where(row_hi == (cell >> 7), spread_w, 0.0).astype(BF16)
            b = onehot(row_lo == (cell & 127)).astype(BF16)
            acc += dot_nt(a, b)
        facc[...] += acc

    rs_out[...] = facc[...].astype(BF16)

    def rs_copy(q):
        return pltpu.make_async_remote_copy(
            src_ref=rs_out.at[pl.ds(pl.multiple_of(sea(q) * 16, 16), 16)],
            dst_ref=rs_in.at[q],
            send_sem=rsend.at[q],
            recv_sem=rrecv.at[q],
            device_id=(atm, sea(q)),
            device_id_type=MESH,
        )

    def ag_copy(q):
        return pltpu.make_async_remote_copy(
            src_ref=table.at[ocn],
            dst_ref=table.at[ocn],
            send_sem=asend.at[q],
            recv_sem=arecv.at[q],
            device_id=(atm, sea(q)),
            device_id_type=MESH,
        )

    for q in range(1, NOCN):
        rs_copy(q).start()
    share = facc[pl.ds(pl.multiple_of(ocn * 16, 16), 16), :]
    for q in range(1, NOCN):
        rs_copy(q).wait()
        share += rs_in[q].astype(F32)
    sea_mask = omask_ref[...].astype(F32)
    rows_out = []
    for s in range(2):
        forcing = jnp.zeros((4, 128), F32)
        for f in range(4):
            forcing += couple_ref[s, f] * share[f * 4 : (f + 1) * 4, :]
        old = jnp.concatenate(
            [ostate_ref[s : s + 1, h * 128 : (h + 1) * 128] for h in range(4)], axis=0
        )
        new = old + sea_mask * jnp.tanh(forcing)
        for h in range(4):
            onew_ref[s : s + 1, h * 128 : (h + 1) * 128] = new[h : h + 1, :]
        rows_out.append(sea_mask * new)
    table[ocn] = jnp.concatenate(rows_out + [sea_mask, jnp.zeros((4, 128), F32)], axis=0)
    for q in range(1, NOCN):
        ag_copy(q).start()

    def msg_wait(i, places):
        msg_copy(i).wait()
        got = msg_in[i]
        both = jnp.concatenate([got & 255, got >> 8], axis=0)
        return places + jnp.where(both > 0, both + (i * MOVE - 1), 0)

    got = msg_out[NPEER]
    both = jnp.concatenate([got & 255, got >> 8], axis=0)
    places = jnp.where(both > 0, both + (NPEER * MOVE - 1), 0)
    q_v[...] = lax.fori_loop(0, NPEER, msg_wait, places)
    q_copy = pltpu.make_async_copy(q_v, q_s, load_sem.at[len(loads) + 1])
    q_copy.start()
    q_copy.wait()
    for q in range(1, NOCN):
        ag_copy(q).wait()
    whole = table[...].reshape(128, 128)
    coarse = whole.astype(BF16)
    fine = (whole - coarse.astype(F32)).astype(BF16)
    split = jnp.concatenate([coarse, fine], axis=1)

    @pl.loop(0, ROWS // CB)
    def _(c):
        cols = pl.ds(pl.multiple_of(c * CB, CB), CB)
        acc = jnp.zeros((16, CB), F32)
        for k in range(4):
            cell = cell_ref[k : k + 1, cols]
            b = onehot(row_lo == (cell & 127)).astype(BF16)
            got = dot(split, jnp.concatenate([b, b], axis=0))
            got = jnp.where(row_hi == (cell >> 7), got, 0.0)
            part = got[0:16]
            for o in range(1, 8):
                part += got[o * 16 : (o + 1) * 16]
            acc += part * weight_ref[k : k + 1, cols]
        rest = 1.0 - jnp.sum(acc[8:12], axis=0, keepdims=True)
        ground = land[:, cols]
        for s in range(2):
            sea_part = jnp.sum(acc[s * 4 : (s + 1) * 4], axis=0, keepdims=True)
            surf_ref[s : s + 1, cols] = sea_part + rest * ground[s : s + 1]

    @pl.loop(0, NPEER)
    def _(i):
        data_copy(i).wait()


def place_kernel(q_s, pool, new_ref, onew_ref, surf_ref, new_out, tend_out, onew_out, surf_out, stage, sem):
    copies = [
        pltpu.make_async_copy(src, dst, sem.at[n])
        for n, (src, dst) in enumerate(
            [(new_ref, new_out), (onew_ref, onew_out), (surf_ref, surf_out)]
        )
    ]
    for copy in copies:
        copy.start()
    def part(n):
        rows = pl.ds(pl.multiple_of(n * PLACE * ND, PLACE * ND), PLACE * ND)
        return pltpu.make_async_copy(stage.at[rows], tend_out.at[rows], sem.at[4 + n])

    @pl.loop(0, NE // PLACE)
    def _(n):
        rows = []
        for j in range(PLACE):
            s = n * PLACE + j
            at = pl.multiple_of(q_s[s // 128, lax.rem(s, 128)] * ND, ND)
            rows.append(pool[pl.ds(at, ND), :])
        block = pl.ds(pl.multiple_of(n * PLACE * ND, PLACE * ND), PLACE * ND)
        stage[block, :] = jnp.concatenate(rows, axis=0)
        part(n).start()

    for copy in copies:
        copy.wait()

    @pl.loop(0, NE // PLACE)
    def _(n):
        part(n).wait()


def body(
    state,
    branch_id,
    span_map,
    derivative,
    rad_weight,
    conv_in,
    conv_out,
    flux_weight,
    remap_cell,
    remap_weight,
    ocean_state,
    ocean_mask,
    couple,
):
    vmem = pl.BlockSpec(memory_space=pltpu.VMEM)
    hbm = pl.BlockSpec(memory_space=pltpu.HBM)
    smem = pl.BlockSpec(memory_space=pltpu.SMEM)
    dma = pltpu.SemaphoreType.DMA
    in_hbm = lambda a: pltpu.with_memory_space_constraint(a, pltpu.HBM)
    stay = lambda a: pltpu.with_memory_space_constraint(a, pltpu.VMEM)
    in_vmem = pltpu.VMEM
    out_hbm = pltpu.HBM
    new_state, pool, places, ocean_new, surface = pl.pallas_call(
        kernel,
        out_shape=(
            in_vmem((ROWS, NF), BF16),
            in_vmem((NPEER * MROWS + NMOVED * ND, NF), BF16),
            pltpu.SMEM((2, 128), I32),
            in_vmem((2, 512), F32),
            in_vmem((2, ROWS), F32),
        ),
        in_specs=[hbm] * 13,
        out_specs=(vmem, vmem, smem, vmem, vmem),
        scratch_shapes=[
            pltpu.VMEM((1, NE), I32),
            pltpu.VMEM((32, 128), I32),
            pltpu.VMEM((ND, ND), BF16),
            pltpu.SMEM((2, 4), F32),
            pltpu.VMEM((4, NF), BF16),
            pltpu.VMEM((4, ROWS), I32),
            pltpu.VMEM((4, ROWS), F32),
            pltpu.VMEM((2, 512), F32),
            pltpu.VMEM((4, 128), I32),
            pltpu.VMEM((ROWS, NF), BF16),
            pltpu.VMEM((NF, 2048), BF16),
            pltpu.VMEM((NF, 2048), BF16),
            pltpu.VMEM((2048, NF), BF16),
            pltpu.VMEM((ROWS, NF), BF16),
            pltpu.VMEM((NE, 128), BF16),
            pltpu.VMEM((NPEER, MROWS, NF), BF16),
            pltpu.VMEM((32, 1, 128), I32),
            pltpu.VMEM((32, 1, 128), I32),
            pltpu.VMEM((8, NE), I32),
            pltpu.SMEM((8, NE), I32),
            pltpu.VMEM((RB, RB), BF16),
            pltpu.VMEM((16, ROWS), F32),
            pltpu.VMEM((16, ROWS), F32),
            pltpu.VMEM((128, 128), F32),
            pltpu.VMEM((128, 128), BF16),
            pltpu.VMEM((NOCN, 16, 128), BF16),
            pltpu.VMEM((NOCN, 16, 128), F32),
            pltpu.SemaphoreType.REGULAR,
            pltpu.VMEM((2, 128), I32),
            dma((15,)),
            dma((NPEER,)),
            dma((NPEER,)),
            dma((NPEER,)),
            dma((NPEER,)),
            dma((NOCN,)),
            dma((NOCN,)),
            dma((NOCN,)),
            dma((NOCN,)),
        ],
        compiler_params=pltpu.CompilerParams(
            collective_id=0, has_side_effects=True, vmem_limit_bytes=32 << 20
        ),
        cost_estimate=pl.CostEstimate(
            flops=14_000_000_000, bytes_accessed=12_000_000, transcendentals=17_000_000
        ),
    )(
        *(
            in_hbm(a)
            for a in (
                span_map.reshape(1, NE),
                branch_id.reshape(32, 128),
                derivative,
                couple.T,
                flux_weight.T,
                remap_cell,
                remap_weight,
                ocean_state,
                ocean_mask.reshape(4, 128),
                state,
                rad_weight,
                conv_in,
                conv_out,
            )
        ),
    )
    new_state, span_tend, ocean_new, surface = pl.pallas_call(
        place_kernel,
        out_shape=(
            out_hbm((ROWS, NF), BF16),
            out_hbm((ROWS, NF), BF16),
            out_hbm((2, 512), F32),
            out_hbm((2, ROWS), F32),
        ),
        in_specs=[smem] + [vmem] * 4,
        out_specs=(hbm,) * 4,
        scratch_shapes=[
            pltpu.VMEM((ROWS, NF), BF16),
            dma((4 + NE // PLACE,)),
        ],
        compiler_params=pltpu.CompilerParams(vmem_limit_bytes=8 << 20),
    )(
        pltpu.with_memory_space_constraint(places, pltpu.SMEM),
        *(stay(a) for a in (pool, new_state, ocean_new, surface)),
    )
    return new_state, span_tend, ocean_new, surface


def solution(mesh):
    cols = P(("atm", "ocn"), None)
    flat = P(("atm", "ocn"))
    lanes = P(None, ("atm", "ocn"))
    return jax.shard_map(
        body,
        mesh=mesh,
        in_specs=(cols, flat, flat, P(), P(), P(), P(), P(), lanes, lanes, lanes, flat, P()),
        out_specs=(cols, cols, lanes, lanes),
        check_vma=False,
    )
```

```python
import jax
import jax.numpy as jnp
from jax import lax
from jax.experimental import pallas as pl
from jax.experimental.pallas import tpu as pltpu
from jax.sharding import PartitionSpec as P

MESH = pl.DeviceIdType.MESH
F32 = jnp.float32
BF16 = jnp.bfloat16
I32 = jnp.int32

NX, NZ = 4, 8
NPEER = NX * NZ - 1
NOCN = 8
NY = 4
NE = 256
ND = 16
NF = 256
ROWS = NE * ND
MOVE = 8
MROWS = MOVE * ND
NMOVED = NE // 2
RB = 256
EB = RB // ND
NB = ROWS // RB
NBM = NMOVED // EB
CB = 512
PLACE = 16


def iota(shape, dim):
    return lax.broadcasted_iota(I32, shape, dim)


def onehot(cond):
    return jnp.where(cond, 1.0, 0.0).astype(F32)


def dot(a, b):
    return jnp.dot(a, b, preferred_element_type=F32)


def dot_nt(a, b):
    return lax.dot_general(a, b, (((1,), (1,)), ((), ())), preferred_element_type=F32)


def column(row):
    parts = [
        jnp.broadcast_to(row[:, h * 128 : (h + 1) * 128], (128, 128)).T for h in range(2)
    ]
    half = jnp.concatenate(parts, axis=0)
    return jnp.concatenate([half, half], axis=1)


def kernel(
    span_hbm,
    branch_hbm,
    deriv_hbm,
    couple_hbm,
    fw_hbm,
    cell_hbm,
    weight_hbm,
    ostate_hbm,
    omask_hbm,
    state_hbm,
    rad_hbm,
    cin_hbm,
    cout_hbm,
    new_ref,
    pool,
    q_s,
    onew_ref,
    surf_ref,
    span_ref,
    branch_ref,
    deriv_ref,
    couple_ref,
    fw_ref,
    cell_ref,
    weight_ref,
    ostate_ref,
    omask_ref,
    state,
    rad,
    cin,
    cout,
    ordered,
    mask_ord,
    send,
    msg_out,
    msg_in,
    scal_v,
    scal_s,
    dblk,
    flux16,
    land,
    facc,
    rs_out,
    rs_in,
    table,
    second,
    q_v,
    load_sem,
    dsend,
    drecv,
    msend,
    mrecv,
    rsend,
    rrecv,
    asend,
    arecv,
):
    atm = lax.axis_index("atm")
    ocn = lax.axis_index("ocn")
    x = atm // NZ
    z = lax.rem(atm, NZ)
    y = ocn // 2
    core = lax.rem(ocn, 2)

    def at_offset(dx, dz):
        return lax.rem(x + dx, NX) * NZ + lax.rem(z + dz, NZ)

    def peer(i):
        rel = i + 1
        return at_offset(rel // NZ, lax.rem(rel, NZ))

    def sea(q):
        return lax.rem(ocn + q, NOCN)

    barrier = pltpu.get_barrier_semaphore()
    along_x = [at_offset(dx, 0) for dx in range(1, NX)]
    along_z = [at_offset(0, dz) for dz in range(1, NZ)]
    along_y = [lax.rem(y + dy, NY) * 2 + core for dy in range(1, NY)]
    mate = y * 2 + 1 - core
    for to in along_z + along_x:
        pl.semaphore_signal(barrier, inc=1, device_id=(to, ocn), device_id_type=MESH)
    for to in along_y + [mate]:
        pl.semaphore_signal(barrier, inc=1, device_id=(atm, to), device_id_type=MESH)
    first_count = len(along_x) + len(along_z) + len(along_y) + 1

    small = [(span_hbm, span_ref), (branch_hbm, branch_ref), (deriv_hbm, deriv_ref)]
    large = [
        (state_hbm, state),
        (rad_hbm, rad),
        (cin_hbm, cin),
        (cout_hbm, cout),
        (fw_hbm, fw_ref),
        (cell_hbm, cell_ref),
        (weight_hbm, weight_ref),
        (ostate_hbm, ostate_ref),
        (omask_hbm, omask_ref),
        (couple_hbm, couple_ref),
    ]
    loads = [
        pltpu.make_async_copy(src, dst, load_sem.at[n])
        for n, (src, dst) in enumerate(small + large)
    ]
    for copy in loads:
        copy.start()
    for copy in loads[: len(small)]:
        copy.wait()

    span = span_ref[...]
    target = span >> 11
    rel = ((((target >> 3) - x) & (NX - 1)) << 3) + (((target & (NZ - 1)) - z) & (NZ - 1))
    key_r = jnp.where(rel == 0, NPEER, rel - 1)
    both_r = key_r * NE + iota((1, NE), 1)
    key_c = column(key_r)
    both_c = column(both_r)
    lane = iota((NE, NE), 1)
    sub = iota((NE, NE), 0)

    def count(cond):
        return jnp.sum(jnp.where(cond, 1, 0), axis=0, keepdims=True)

    pos_r = count(both_c < both_r)
    src_r = jnp.sum(jnp.where(column(pos_r) == lane, sub, 0), axis=0, keepdims=True)
    scal_v[0:1, :] = src_r
    scal_v[1:2, :] = pos_r
    scal_v[2:3, :] = jnp.minimum(count(key_c < lane), NMOVED)
    scal_copy = pltpu.make_async_copy(scal_v, scal_s, load_sem.at[len(loads)])
    scal_copy.start()
    rank_r = jnp.where(key_r == NPEER, pos_r - (NMOVED - 1), pos_r - count(key_c < key_r) + 1)
    pick = jnp.where(key_r == iota((32, NE), 0), rank_r, 0).astype(F32).astype(BF16)
    slots = onehot(column(span & (NE - 1)) == lane).astype(BF16)
    msg = dot(pick, slots)
    packed = (msg[:, :128] + 256.0 * msg[:, 128:]).astype(I32)
    for i in range(32):
        msg_out[i] = packed[i : i + 1, :]
    bits = branch_ref[...].astype(F32).astype(BF16)
    spread = dot(onehot(iota((NE, 32), 0) // 8 == iota((NE, 32), 1)).astype(BF16), bits)
    own = jnp.where(iota((NE, 128), 1) // ND == iota((NE, 128), 0) % 8, spread, 0.0)
    fold = onehot(iota((128, 128), 0) % ND == iota((128, 128), 1) % ND).astype(BF16)
    bits_nat = dot(own.astype(BF16), fold).astype(BF16)
    order = onehot(pos_r == sub).astype(BF16)
    mask_ord[...] = dot(order, bits_nat).astype(BF16)
    spread_rows = onehot(iota((RB, ND), 0) % ND == iota((RB, ND), 1)).astype(BF16)
    tiled = dot_nt(dot(spread_rows, deriv_ref[...]).astype(BF16), spread_rows)
    same = iota((RB, RB), 0) // ND == iota((RB, RB), 1) // ND
    dblk[...] = jnp.where(same, tiled, 0.0).astype(BF16)
    for copy in loads[len(small) :]:
        copy.wait()
    scal_copy.wait()

    to_rows = onehot(iota((RB, EB), 0) // ND == iota((RB, EB), 1)).astype(BF16)
    my_lane = iota((RB, 128), 1) == iota((RB, 128), 0) % ND
    ones = jnp.ones((128, NF), BF16)

    def gather(ref, row, b):
        rows = [ref[pl.ds(scal_s[row, b * EB + j] * ND, ND), :] for j in range(EB)]
        return jnp.concatenate(rows, axis=0)

    def physics(b):
        cols = gather(state, 0, b)
        total = jnp.zeros((RB, NF), F32)
        conv = jnp.zeros((RB, NF), F32)
        for g in range(8):
            part = slice(g * NF, (g + 1) * NF)
            total += jnp.tanh(dot(cols, rad[:, part]))
            half = 0.5 * dot(cols, cin[:, part])
            hidden = (half * (1.0 + jnp.tanh(half))).astype(BF16)
            conv += dot(hidden, cout[part, :])
        bits_b = mask_ord[pl.ds(pl.multiple_of(b * EB, EB), EB), :]
        mine = jnp.where(my_lane, dot(to_rows, bits_b), 0.0).astype(BF16)
        mask = dot(mine, ones)
        out = (0.25 * total + mask * conv).astype(BF16)
        ordered[pl.ds(pl.multiple_of(b * RB, RB), RB), :] = out

    def data_copy(i):
        return pltpu.make_async_remote_copy(
            src_ref=send.at[i],
            dst_ref=pool.at[pl.ds(pl.multiple_of(i * MROWS, MROWS), MROWS)],
            send_sem=dsend.at[i],
            recv_sem=drecv.at[i],
            device_id=(peer(i), ocn),
            device_id_type=MESH,
        )

    def msg_copy(i):
        return pltpu.make_async_remote_copy(
            src_ref=msg_out.at[i],
            dst_ref=msg_in.at[i],
            send_sem=msend.at[i],
            recv_sem=mrecv.at[i],
            device_id=(peer(i), ocn),
            device_id_type=MESH,
        )

    def ship(i):
        at = scal_s[2, i] * ND
        send[i] = ordered[pl.ds(at, MROWS), :]
        data_copy(i).start()

    per_block = EB // MOVE

    @pl.loop(0, NB)
    def _(b):
        physics(b)

        @pl.when(b == 0)
        def _():
            pl.semaphore_wait(barrier, first_count)

        @pl.when(b == 3)
        def _():
            pl.semaphore_wait(second, len(along_x) + 1)

            @pl.loop(0, NPEER)
            def _(i):
                msg_copy(i).start()

        @pl.when(b < NBM)
        def _():
            for i in range(per_block):
                ship(b * per_block + i)

        @pl.when(b == 0)
        def _():
            for to in along_x:
                pl.semaphore_signal(second, inc=1, device_id=(to, ocn), device_id_type=MESH)
            pl.semaphore_signal(second, inc=1, device_id=(atm, mate), device_id_type=MESH)

        @pl.when(b == NBM - 1)
        def _():
            @pl.loop(NBM * per_block, NPEER)
            def _(i):
                ship(i)

    @pl.loop(0, NB - NBM)
    def _(n):
        at = pl.ds(pl.multiple_of(NPEER * MROWS + n * RB, MROWS), RB)
        pool[at, :] = ordered[pl.ds(pl.multiple_of((NBM + n) * RB, RB), RB), :]

    rep = onehot(iota((16, 4), 0) // 4 == iota((16, 4), 1)).astype(BF16)
    fw16 = dot(rep, fw_ref[...]).astype(BF16)
    level = jnp.where(iota((16, NF), 0) == 0, NF // 2 - 1, NF - 1)
    ends = onehot((iota((16, NF), 1) == level) & (iota((16, NF), 0) < 2)).astype(BF16)

    @pl.loop(0, NB)
    def _(b):
        tend = gather(ordered, 1, b)
        rows = pl.ds(pl.multiple_of(b * RB, RB), RB)
        old = state[rows, :]
        new = (old.astype(F32) + dot(dblk[...], old) + tend.astype(F32)).astype(BF16)
        new_ref[rows, :] = new
        flux16[:, rows] = dot_nt(fw16, tend)
        land[:, rows] = dot_nt(ends, new)

    row_hi = (iota((128, CB), 0) // 16) * 4 + iota((128, CB), 0) % 4
    row_lo = iota((128, CB), 0)
    facc[...] = jnp.zeros((128, 128), F32)

    @pl.loop(0, ROWS // CB)
    def _(c):
        cols = pl.ds(pl.multiple_of(c * CB, CB), CB)
        vals = flux16[:, cols]
        acc = jnp.zeros((128, 128), F32)
        for k in range(4):
            cell = cell_ref[k : k + 1, cols]
            weighted = vals * weight_ref[k : k + 1, cols]
            spread_w = jnp.concatenate([weighted] * 8, axis=0)
            a = jnp.where(row_hi == (cell >> 7), spread_w, 0.0).astype(BF16)
            b = onehot(row_lo == (cell & 127)).astype(BF16)
            acc += dot_nt(a, b)
        facc[...] += acc

    rs_out[...] = facc[...].astype(BF16)

    def rs_copy(q):
        return pltpu.make_async_remote_copy(
            src_ref=rs_out.at[pl.ds(pl.multiple_of(sea(q) * 16, 16), 16)],
            dst_ref=rs_in.at[q],
            send_sem=rsend.at[q],
            recv_sem=rrecv.at[q],
            device_id=(atm, sea(q)),
            device_id_type=MESH,
        )

    def ag_copy(q):
        return pltpu.make_async_remote_copy(
            src_ref=table.at[ocn],
            dst_ref=table.at[ocn],
            send_sem=asend.at[q],
            recv_sem=arecv.at[q],
            device_id=(atm, sea(q)),
            device_id_type=MESH,
        )

    for q in range(1, NOCN):
        rs_copy(q).start()
    share = facc[pl.ds(pl.multiple_of(ocn * 16, 16), 16), :]
    for q in range(1, NOCN):
        rs_copy(q).wait()
        share += rs_in[q].astype(F32)
    sea_mask = omask_ref[...].astype(F32)
    rows_out = []
    for s in range(2):
        forcing = jnp.zeros((4, 128), F32)
        for f in range(4):
            forcing += couple_ref[s, f] * share[f * 4 : (f + 1) * 4, :]
        old = jnp.concatenate(
            [ostate_ref[s : s + 1, h * 128 : (h + 1) * 128] for h in range(4)], axis=0
        )
        new = old + sea_mask * jnp.tanh(forcing)
        for h in range(4):
            onew_ref[s : s + 1, h * 128 : (h + 1) * 128] = new[h : h + 1, :]
        rows_out.append(sea_mask * new)
    table[ocn] = jnp.concatenate(rows_out + [sea_mask, jnp.zeros((4, 128), F32)], axis=0)
    for q in range(1, NOCN):
        ag_copy(q).start()

    def msg_wait(i, places):
        msg_copy(i).wait()
        got = msg_in[i]
        both = jnp.concatenate([got & 255, got >> 8], axis=0)
        return places + jnp.where(both > 0, both + (i * MOVE - 1), 0)

    got = msg_out[NPEER]
    both = jnp.concatenate([got & 255, got >> 8], axis=0)
    places = jnp.where(both > 0, both + (NPEER * MOVE - 1), 0)
    q_v[...] = lax.fori_loop(0, NPEER, msg_wait, places)
    q_copy = pltpu.make_async_copy(q_v, q_s, load_sem.at[len(loads) + 1])
    q_copy.start()
    q_copy.wait()
    for q in range(1, NOCN):
        ag_copy(q).wait()
    whole = table[...].reshape(128, 128)
    coarse = whole.astype(BF16)
    fine = (whole - coarse.astype(F32)).astype(BF16)
    split = jnp.concatenate([coarse, fine], axis=1)

    @pl.loop(0, ROWS // CB)
    def _(c):
        cols = pl.ds(pl.multiple_of(c * CB, CB), CB)
        acc = jnp.zeros((16, CB), F32)
        for k in range(4):
            cell = cell_ref[k : k + 1, cols]
            b = onehot(row_lo == (cell & 127)).astype(BF16)
            got = dot(split, jnp.concatenate([b, b], axis=0))
            got = jnp.where(row_hi == (cell >> 7), got, 0.0)
            part = got[0:16]
            for o in range(1, 8):
                part += got[o * 16 : (o + 1) * 16]
            acc += part * weight_ref[k : k + 1, cols]
        rest = 1.0 - jnp.sum(acc[8:12], axis=0, keepdims=True)
        ground = land[:, cols]
        for s in range(2):
            sea_part = jnp.sum(acc[s * 4 : (s + 1) * 4], axis=0, keepdims=True)
            surf_ref[s : s + 1, cols] = sea_part + rest * ground[s : s + 1]

    @pl.loop(0, NPEER)
    def _(i):
        data_copy(i).wait()


def place_kernel(q_s, pool, new_ref, onew_ref, surf_ref, new_out, tend_out, onew_out, surf_out, stage, sem):
    copies = [
        pltpu.make_async_copy(src, dst, sem.at[n])
        for n, (src, dst) in enumerate(
            [(new_ref, new_out), (onew_ref, onew_out), (surf_ref, surf_out)]
        )
    ]
    for copy in copies:
        copy.start()
    def part(n):
        rows = pl.ds(pl.multiple_of(n * PLACE * ND, PLACE * ND), PLACE * ND)
        return pltpu.make_async_copy(stage.at[rows], tend_out.at[rows], sem.at[4 + n])

    @pl.loop(0, NE // PLACE)
    def _(n):
        rows = []
        for j in range(PLACE):
            s = n * PLACE + j
            at = pl.multiple_of(q_s[s // 128, lax.rem(s, 128)] * ND, ND)
            rows.append(pool[pl.ds(at, ND), :])
        block = pl.ds(pl.multiple_of(n * PLACE * ND, PLACE * ND), PLACE * ND)
        stage[block, :] = jnp.concatenate(rows, axis=0)
        part(n).start()

    for copy in copies:
        copy.wait()

    @pl.loop(0, NE // PLACE)
    def _(n):
        part(n).wait()


def body(
    state,
    branch_id,
    span_map,
    derivative,
    rad_weight,
    conv_in,
    conv_out,
    flux_weight,
    remap_cell,
    remap_weight,
    ocean_state,
    ocean_mask,
    couple,
):
    vmem = pl.BlockSpec(memory_space=pltpu.VMEM)
    hbm = pl.BlockSpec(memory_space=pltpu.HBM)
    smem = pl.BlockSpec(memory_space=pltpu.SMEM)
    dma = pltpu.SemaphoreType.DMA
    in_hbm = lambda a: pltpu.with_memory_space_constraint(a, pltpu.HBM)
    stay = lambda a: pltpu.with_memory_space_constraint(a, pltpu.VMEM)
    in_vmem = pltpu.VMEM
    out_hbm = pltpu.HBM
    new_state, pool, places, ocean_new, surface = pl.pallas_call(
        kernel,
        out_shape=(
            in_vmem((ROWS, NF), BF16),
            in_vmem((NPEER * MROWS + NMOVED * ND, NF), BF16),
            pltpu.SMEM((2, 128), I32),
            in_vmem((2, 512), F32),
            in_vmem((2, ROWS), F32),
        ),
        in_specs=[hbm] * 13,
        out_specs=(vmem, vmem, smem, vmem, vmem),
        scratch_shapes=[
            pltpu.VMEM((1, NE), I32),
            pltpu.VMEM((32, 128), I32),
            pltpu.VMEM((ND, ND), BF16),
            pltpu.SMEM((2, 4), F32),
            pltpu.VMEM((4, NF), BF16),
            pltpu.VMEM((4, ROWS), I32),
            pltpu.VMEM((4, ROWS), F32),
            pltpu.VMEM((2, 512), F32),
            pltpu.VMEM((4, 128), I32),
            pltpu.VMEM((ROWS, NF), BF16),
            pltpu.VMEM((NF, 2048), BF16),
            pltpu.VMEM((NF, 2048), BF16),
            pltpu.VMEM((2048, NF), BF16),
            pltpu.VMEM((ROWS, NF), BF16),
            pltpu.VMEM((NE, 128), BF16),
            pltpu.VMEM((NPEER, MROWS, NF), BF16),
            pltpu.VMEM((32, 1, 128), I32),
            pltpu.VMEM((32, 1, 128), I32),
            pltpu.VMEM((8, NE), I32),
            pltpu.SMEM((8, NE), I32),
            pltpu.VMEM((RB, RB), BF16),
            pltpu.VMEM((16, ROWS), F32),
            pltpu.VMEM((16, ROWS), F32),
            pltpu.VMEM((128, 128), F32),
            pltpu.VMEM((128, 128), BF16),
            pltpu.VMEM((NOCN, 16, 128), BF16),
            pltpu.VMEM((NOCN, 16, 128), F32),
            pltpu.SemaphoreType.REGULAR,
            pltpu.VMEM((2, 128), I32),
            dma((15,)),
            dma((NPEER,)),
            dma((NPEER,)),
            dma((NPEER,)),
            dma((NPEER,)),
            dma((NOCN,)),
            dma((NOCN,)),
            dma((NOCN,)),
            dma((NOCN,)),
        ],
        compiler_params=pltpu.CompilerParams(
            collective_id=0, has_side_effects=True, vmem_limit_bytes=32 << 20
        ),
        cost_estimate=pl.CostEstimate(
            flops=14_000_000_000, bytes_accessed=12_000_000, transcendentals=17_000_000
        ),
    )(
        *(
            in_hbm(a)
            for a in (
                span_map.reshape(1, NE),
                branch_id.reshape(32, 128),
                derivative,
                couple.T,
                flux_weight.T,
                remap_cell,
                remap_weight,
                ocean_state,
                ocean_mask.reshape(4, 128),
                state,
                rad_weight,
                conv_in,
                conv_out,
            )
        ),
    )
    new_state, span_tend, ocean_new, surface = pl.pallas_call(
        place_kernel,
        out_shape=(
            out_hbm((ROWS, NF), BF16),
            out_hbm((ROWS, NF), BF16),
            out_hbm((2, 512), F32),
            out_hbm((2, ROWS), F32),
        ),
        in_specs=[smem] + [vmem] * 4,
        out_specs=(hbm,) * 4,
        scratch_shapes=[
            pltpu.VMEM((ROWS, NF), BF16),
            dma((4 + NE // PLACE,)),
        ],
        compiler_params=pltpu.CompilerParams(vmem_limit_bytes=8 << 20),
    )(
        pltpu.with_memory_space_constraint(places, pltpu.SMEM),
        *(stay(a) for a in (pool, new_state, ocean_new, surface)),
    )
    return new_state, span_tend, ocean_new, surface


def solution(mesh):
    cols = P(("atm", "ocn"), None)
    flat = P(("atm", "ocn"))
    lanes = P(None, ("atm", "ocn"))
    return jax.shard_map(
        body,
        mesh=mesh,
        in_specs=(cols, flat, flat, P(), P(), P(), P(), P(), lanes, lanes, lanes, flat, P()),
        out_specs=(cols, cols, lanes, lanes),
        check_vma=False,
    )
```

```python
import jax
import jax.numpy as jnp
from jax import lax
from jax.experimental import pallas as pl
from jax.experimental.pallas import tpu as pltpu
from jax.sharding import PartitionSpec as P

MESH = pl.DeviceIdType.MESH
F32 = jnp.float32
BF16 = jnp.bfloat16
I32 = jnp.int32

NX, NZ = 4, 8
NPEER = NX * NZ - 1
NOCN = 8
NY = 4
NE = 256
ND = 16
NF = 256
ROWS = NE * ND
MOVE = 8
MROWS = MOVE * ND
NMOVED = NE // 2
RB = 256
EB = RB // ND
NB = ROWS // RB
NBM = NMOVED // EB
CB = 512
PLACE = 32


def iota(shape, dim):
    return lax.broadcasted_iota(I32, shape, dim)


def onehot(cond):
    return jnp.where(cond, 1.0, 0.0).astype(F32)


def dot(a, b):
    return jnp.dot(a, b, preferred_element_type=F32)


def dot_nt(a, b):
    return lax.dot_general(a, b, (((1,), (1,)), ((), ())), preferred_element_type=F32)


def column(row):
    parts = [
        jnp.broadcast_to(row[:, h * 128 : (h + 1) * 128], (128, 128)).T for h in range(2)
    ]
    half = jnp.concatenate(parts, axis=0)
    return jnp.concatenate([half, half], axis=1)


def kernel(
    span_hbm,
    branch_hbm,
    deriv_hbm,
    couple_hbm,
    fw_hbm,
    cell_hbm,
    weight_hbm,
    ostate_hbm,
    omask_hbm,
    state_hbm,
    rad_hbm,
    cin_hbm,
    cout_hbm,
    new_ref,
    pool,
    q_s,
    onew_ref,
    surf_ref,
    span_ref,
    branch_ref,
    deriv_ref,
    couple_ref,
    fw_ref,
    cell_ref,
    weight_ref,
    ostate_ref,
    omask_ref,
    state,
    rad,
    cin,
    cout,
    ordered,
    mask_ord,
    send,
    msg_out,
    msg_in,
    scal_v,
    scal_s,
    dblk,
    flux16,
    land,
    facc,
    rs_out,
    rs_in,
    table,
    second,
    q_v,
    load_sem,
    dsend,
    drecv,
    msend,
    mrecv,
    rsend,
    rrecv,
    asend,
    arecv,
):
    atm = lax.axis_index("atm")
    ocn = lax.axis_index("ocn")
    x = atm // NZ
    z = lax.rem(atm, NZ)
    y = ocn // 2
    core = lax.rem(ocn, 2)

    def at_offset(dx, dz):
        return lax.rem(x + dx, NX) * NZ + lax.rem(z + dz, NZ)

    def peer(i):
        rel = i + 1
        return at_offset(rel // NZ, lax.rem(rel, NZ))

    def sea(q):
        return lax.rem(ocn + q, NOCN)

    barrier = pltpu.get_barrier_semaphore()
    along_x = [at_offset(dx, 0) for dx in range(1, NX)]
    along_z = [at_offset(0, dz) for dz in range(1, NZ)]
    along_y = [lax.rem(y + dy, NY) * 2 + core for dy in range(1, NY)]
    mate = y * 2 + 1 - core
    for to in along_z + along_x:
        pl.semaphore_signal(barrier, inc=1, device_id=(to, ocn), device_id_type=MESH)
    for to in along_y + [mate]:
        pl.semaphore_signal(barrier, inc=1, device_id=(atm, to), device_id_type=MESH)
    first_count = len(along_x) + len(along_z) + len(along_y) + 1

    small = [(span_hbm, span_ref), (branch_hbm, branch_ref), (deriv_hbm, deriv_ref)]
    large = [
        (state_hbm, state),
        (rad_hbm, rad),
        (cin_hbm, cin),
        (cout_hbm, cout),
        (fw_hbm, fw_ref),
        (cell_hbm, cell_ref),
        (weight_hbm, weight_ref),
        (ostate_hbm, ostate_ref),
        (omask_hbm, omask_ref),
        (couple_hbm, couple_ref),
    ]
    loads = [
        pltpu.make_async_copy(src, dst, load_sem.at[n])
        for n, (src, dst) in enumerate(small + large)
    ]
    for copy in loads:
        copy.start()
    for copy in loads[: len(small)]:
        copy.wait()

    span = span_ref[...]
    target = span >> 11
    rel = ((((target >> 3) - x) & (NX - 1)) << 3) + (((target & (NZ - 1)) - z) & (NZ - 1))
    key_r = jnp.where(rel == 0, NPEER, rel - 1)
    both_r = key_r * NE + iota((1, NE), 1)
    key_c = column(key_r)
    both_c = column(both_r)
    lane = iota((NE, NE), 1)
    sub = iota((NE, NE), 0)

    def count(cond):
        return jnp.sum(jnp.where(cond, 1, 0), axis=0, keepdims=True)

    pos_r = count(both_c < both_r)
    src_r = jnp.sum(jnp.where(column(pos_r) == lane, sub, 0), axis=0, keepdims=True)
    scal_v[0:1, :] = src_r
    scal_v[1:2, :] = pos_r
    scal_v[2:3, :] = jnp.minimum(count(key_c < lane), NMOVED)
    scal_copy = pltpu.make_async_copy(scal_v, scal_s, load_sem.at[len(loads)])
    scal_copy.start()
    rank_r = jnp.where(key_r == NPEER, pos_r - (NMOVED - 1), pos_r - count(key_c < key_r) + 1)
    pick = jnp.where(key_r == iota((32, NE), 0), rank_r, 0).astype(F32).astype(BF16)
    slots = onehot(column(span & (NE - 1)) == lane).astype(BF16)
    msg = dot(pick, slots)
    packed = (msg[:, :128] + 256.0 * msg[:, 128:]).astype(I32)
    for i in range(32):
        msg_out[i] = packed[i : i + 1, :]
    bits = branch_ref[...].astype(F32).astype(BF16)
    spread = dot(onehot(iota((NE, 32), 0) // 8 == iota((NE, 32), 1)).astype(BF16), bits)
    own = jnp.where(iota((NE, 128), 1) // ND == iota((NE, 128), 0) % 8, spread, 0.0)
    fold = onehot(iota((128, 128), 0) % ND == iota((128, 128), 1) % ND).astype(BF16)
    bits_nat = dot(own.astype(BF16), fold).astype(BF16)
    order = onehot(pos_r == sub).astype(BF16)
    mask_ord[...] = dot(order, bits_nat).astype(BF16)
    spread_rows = onehot(iota((RB, ND), 0) % ND == iota((RB, ND), 1)).astype(BF16)
    tiled = dot_nt(dot(spread_rows, deriv_ref[...]).astype(BF16), spread_rows)
    same = iota((RB, RB), 0) // ND == iota((RB, RB), 1) // ND
    dblk[...] = jnp.where(same, tiled, 0.0).astype(BF16)
    for copy in loads[len(small) :]:
        copy.wait()
    scal_copy.wait()

    to_rows = onehot(iota((RB, EB), 0) // ND == iota((RB, EB), 1)).astype(BF16)
    my_lane = iota((RB, 128), 1) == iota((RB, 128), 0) % ND
    ones = jnp.ones((128, NF), BF16)

    def gather(ref, row, b):
        rows = [ref[pl.ds(scal_s[row, b * EB + j] * ND, ND), :] for j in range(EB)]
        return jnp.concatenate(rows, axis=0)

    def physics(b):
        cols = gather(state, 0, b)
        total = jnp.zeros((RB, NF), F32)
        conv = jnp.zeros((RB, NF), F32)
        for g in range(8):
            part = slice(g * NF, (g + 1) * NF)
            total += jnp.tanh(dot(cols, rad[:, part]))
            half = 0.5 * dot(cols, cin[:, part])
            hidden = (half * (1.0 + jnp.tanh(half))).astype(BF16)
            conv += dot(hidden, cout[part, :])
        bits_b = mask_ord[pl.ds(pl.multiple_of(b * EB, EB), EB), :]
        mine = jnp.where(my_lane, dot(to_rows, bits_b), 0.0).astype(BF16)
        mask = dot(mine, ones)
        out = (0.25 * total + mask * conv).astype(BF16)
        ordered[pl.ds(pl.multiple_of(b * RB, RB), RB), :] = out

    def data_copy(i):
        return pltpu.make_async_remote_copy(
            src_ref=send.at[i],
            dst_ref=pool.at[pl.ds(pl.multiple_of(i * MROWS, MROWS), MROWS)],
            send_sem=dsend.at[i],
            recv_sem=drecv.at[i],
            device_id=(peer(i), ocn),
            device_id_type=MESH,
        )

    def msg_copy(i):
        return pltpu.make_async_remote_copy(
            src_ref=msg_out.at[i],
            dst_ref=msg_in.at[i],
            send_sem=msend.at[i],
            recv_sem=mrecv.at[i],
            device_id=(peer(i), ocn),
            device_id_type=MESH,
        )

    def ship(i):
        at = scal_s[2, i] * ND
        send[i] = ordered[pl.ds(at, MROWS), :]
        data_copy(i).start()

    per_block = EB // MOVE

    @pl.loop(0, NB)
    def _(b):
        physics(b)

        @pl.when(b == 0)
        def _():
            pl.semaphore_wait(barrier, first_count)
            for to in along_x:
                pl.semaphore_signal(second, inc=1, device_id=(to, ocn), device_id_type=MESH)
            pl.semaphore_signal(second, inc=1, device_id=(atm, mate), device_id_type=MESH)

        @pl.when(b == 3)
        def _():
            pl.semaphore_wait(second, len(along_x) + 1)

            @pl.loop(0, NPEER)
            def _(i):
                msg_copy(i).start()

        @pl.when(b < NBM)
        def _():
            for i in range(per_block):
                ship(b * per_block + i)

        @pl.when(b == NBM - 1)
        def _():
            @pl.loop(NBM * per_block, NPEER)
            def _(i):
                ship(i)

    @pl.loop(0, NB - NBM)
    def _(n):
        at = pl.ds(pl.multiple_of(NPEER * MROWS + n * RB, MROWS), RB)
        pool[at, :] = ordered[pl.ds(pl.multiple_of((NBM + n) * RB, RB), RB), :]

    rep = onehot(iota((16, 4), 0) // 4 == iota((16, 4), 1)).astype(BF16)
    fw16 = dot(rep, fw_ref[...]).astype(BF16)
    level = jnp.where(iota((16, NF), 0) == 0, NF // 2 - 1, NF - 1)
    ends = onehot((iota((16, NF), 1) == level) & (iota((16, NF), 0) < 2)).astype(BF16)

    @pl.loop(0, NB)
    def _(b):
        tend = gather(ordered, 1, b)
        rows = pl.ds(pl.multiple_of(b * RB, RB), RB)
        old = state[rows, :]
        new = (old.astype(F32) + dot(dblk[...], old) + tend.astype(F32)).astype(BF16)
        new_ref[rows, :] = new
        flux16[:, rows] = dot_nt(fw16, tend)
        land[:, rows] = dot_nt(ends, new)

    row_hi = (iota((128, CB), 0) // 16) * 4 + iota((128, CB), 0) % 4
    row_lo = iota((128, CB), 0)
    facc[...] = jnp.zeros((128, 128), F32)

    @pl.loop(0, ROWS // CB)
    def _(c):
        cols = pl.ds(pl.multiple_of(c * CB, CB), CB)
        vals = flux16[:, cols]
        acc = jnp.zeros((128, 128), F32)
        for k in range(4):
            cell = cell_ref[k : k + 1, cols]
            weighted = vals * weight_ref[k : k + 1, cols]
            spread_w = jnp.concatenate([weighted] * 8, axis=0)
            a = jnp.where(row_hi == (cell >> 7), spread_w, 0.0).astype(BF16)
            b = onehot(row_lo == (cell & 127)).astype(BF16)
            acc += dot_nt(a, b)
        facc[...] += acc

    rs_out[...] = facc[...].astype(BF16)

    def rs_copy(q):
        return pltpu.make_async_remote_copy(
            src_ref=rs_out.at[pl.ds(pl.multiple_of(sea(q) * 16, 16), 16)],
            dst_ref=rs_in.at[q],
            send_sem=rsend.at[q],
            recv_sem=rrecv.at[q],
            device_id=(atm, sea(q)),
            device_id_type=MESH,
        )

    def ag_copy(q):
        return pltpu.make_async_remote_copy(
            src_ref=table.at[ocn],
            dst_ref=table.at[ocn],
            send_sem=asend.at[q],
            recv_sem=arecv.at[q],
            device_id=(atm, sea(q)),
            device_id_type=MESH,
        )

    for q in range(1, NOCN):
        rs_copy(q).start()
    share = facc[pl.ds(pl.multiple_of(ocn * 16, 16), 16), :]
    for q in range(1, NOCN):
        rs_copy(q).wait()
        share += rs_in[q].astype(F32)
    sea_mask = omask_ref[...].astype(F32)
    rows_out = []
    for s in range(2):
        forcing = jnp.zeros((4, 128), F32)
        for f in range(4):
            forcing += couple_ref[s, f] * share[f * 4 : (f + 1) * 4, :]
        old = jnp.concatenate(
            [ostate_ref[s : s + 1, h * 128 : (h + 1) * 128] for h in range(4)], axis=0
        )
        new = old + sea_mask * jnp.tanh(forcing)
        for h in range(4):
            onew_ref[s : s + 1, h * 128 : (h + 1) * 128] = new[h : h + 1, :]
        rows_out.append(sea_mask * new)
    table[ocn] = jnp.concatenate(rows_out + [sea_mask, jnp.zeros((4, 128), F32)], axis=0)
    for q in range(1, NOCN):
        ag_copy(q).start()

    def msg_wait(i, places):
        msg_copy(i).wait()
        got = msg_in[i]
        both = jnp.concatenate([got & 255, got >> 8], axis=0)
        return places + jnp.where(both > 0, both + (i * MOVE - 1), 0)

    got = msg_out[NPEER]
    both = jnp.concatenate([got & 255, got >> 8], axis=0)
    places = jnp.where(both > 0, both + (NPEER * MOVE - 1), 0)
    q_v[...] = lax.fori_loop(0, NPEER, msg_wait, places)
    q_copy = pltpu.make_async_copy(q_v, q_s, load_sem.at[len(loads) + 1])
    q_copy.start()
    q_copy.wait()
    for q in range(1, NOCN):
        ag_copy(q).wait()
    whole = table[...].reshape(128, 128)
    coarse = whole.astype(BF16)
    fine = (whole - coarse.astype(F32)).astype(BF16)
    split = jnp.concatenate([coarse, fine], axis=1)

    @pl.loop(0, ROWS // CB)
    def _(c):
        cols = pl.ds(pl.multiple_of(c * CB, CB), CB)
        acc = jnp.zeros((16, CB), F32)
        for k in range(4):
            cell = cell_ref[k : k + 1, cols]
            b = onehot(row_lo == (cell & 127)).astype(BF16)
            got = dot(split, jnp.concatenate([b, b], axis=0))
            got = jnp.where(row_hi == (cell >> 7), got, 0.0)
            part = got[0:16]
            for o in range(1, 8):
                part += got[o * 16 : (o + 1) * 16]
            acc += part * weight_ref[k : k + 1, cols]
        rest = 1.0 - jnp.sum(acc[8:12], axis=0, keepdims=True)
        ground = land[:, cols]
        for s in range(2):
            sea_part = jnp.sum(acc[s * 4 : (s + 1) * 4], axis=0, keepdims=True)
            surf_ref[s : s + 1, cols] = sea_part + rest * ground[s : s + 1]

    @pl.loop(0, NPEER)
    def _(i):
        data_copy(i).wait()


def place_kernel(q_s, pool, new_ref, onew_ref, surf_ref, new_out, tend_out, onew_out, surf_out, stage, sem):
    copies = [
        pltpu.make_async_copy(src, dst, sem.at[n])
        for n, (src, dst) in enumerate(
            [(new_ref, new_out), (onew_ref, onew_out), (surf_ref, surf_out)]
        )
    ]
    for copy in copies:
        copy.start()
    def part(n):
        rows = pl.ds(pl.multiple_of(n * PLACE * ND, PLACE * ND), PLACE * ND)
        return pltpu.make_async_copy(stage.at[rows], tend_out.at[rows], sem.at[4 + n])

    @pl.loop(0, NE // PLACE)
    def _(n):
        rows = []
        for j in range(PLACE):
            s = n * PLACE + j
            at = pl.multiple_of(q_s[s // 128, lax.rem(s, 128)] * ND, ND)
            rows.append(pool[pl.ds(at, ND), :])
        block = pl.ds(pl.multiple_of(n * PLACE * ND, PLACE * ND), PLACE * ND)
        stage[block, :] = jnp.concatenate(rows, axis=0)
        part(n).start()

    for copy in copies:
        copy.wait()

    @pl.loop(0, NE // PLACE)
    def _(n):
        part(n).wait()


def body(
    state,
    branch_id,
    span_map,
    derivative,
    rad_weight,
    conv_in,
    conv_out,
    flux_weight,
    remap_cell,
    remap_weight,
    ocean_state,
    ocean_mask,
    couple,
):
    vmem = pl.BlockSpec(memory_space=pltpu.VMEM)
    hbm = pl.BlockSpec(memory_space=pltpu.HBM)
    smem = pl.BlockSpec(memory_space=pltpu.SMEM)
    dma = pltpu.SemaphoreType.DMA
    in_hbm = lambda a: pltpu.with_memory_space_constraint(a, pltpu.HBM)
    stay = lambda a: pltpu.with_memory_space_constraint(a, pltpu.VMEM)
    in_vmem = pltpu.VMEM
    out_hbm = pltpu.HBM
    new_state, pool, places, ocean_new, surface = pl.pallas_call(
        kernel,
        out_shape=(
            in_vmem((ROWS, NF), BF16),
            in_vmem((NPEER * MROWS + NMOVED * ND, NF), BF16),
            pltpu.SMEM((2, 128), I32),
            in_vmem((2, 512), F32),
            in_vmem((2, ROWS), F32),
        ),
        in_specs=[hbm] * 13,
        out_specs=(vmem, vmem, smem, vmem, vmem),
        scratch_shapes=[
            pltpu.VMEM((1, NE), I32),
            pltpu.VMEM((32, 128), I32),
            pltpu.VMEM((ND, ND), BF16),
            pltpu.SMEM((2, 4), F32),
            pltpu.VMEM((4, NF), BF16),
            pltpu.VMEM((4, ROWS), I32),
            pltpu.VMEM((4, ROWS), F32),
            pltpu.VMEM((2, 512), F32),
            pltpu.VMEM((4, 128), I32),
            pltpu.VMEM((ROWS, NF), BF16),
            pltpu.VMEM((NF, 2048), BF16),
            pltpu.VMEM((NF, 2048), BF16),
            pltpu.VMEM((2048, NF), BF16),
            pltpu.VMEM((ROWS, NF), BF16),
            pltpu.VMEM((NE, 128), BF16),
            pltpu.VMEM((NPEER, MROWS, NF), BF16),
            pltpu.VMEM((32, 1, 128), I32),
            pltpu.VMEM((32, 1, 128), I32),
            pltpu.VMEM((8, NE), I32),
            pltpu.SMEM((8, NE), I32),
            pltpu.VMEM((RB, RB), BF16),
            pltpu.VMEM((16, ROWS), F32),
            pltpu.VMEM((16, ROWS), F32),
            pltpu.VMEM((128, 128), F32),
            pltpu.VMEM((128, 128), BF16),
            pltpu.VMEM((NOCN, 16, 128), BF16),
            pltpu.VMEM((NOCN, 16, 128), F32),
            pltpu.SemaphoreType.REGULAR,
            pltpu.VMEM((2, 128), I32),
            dma((15,)),
            dma((NPEER,)),
            dma((NPEER,)),
            dma((NPEER,)),
            dma((NPEER,)),
            dma((NOCN,)),
            dma((NOCN,)),
            dma((NOCN,)),
            dma((NOCN,)),
        ],
        compiler_params=pltpu.CompilerParams(
            collective_id=0, has_side_effects=True, vmem_limit_bytes=32 << 20
        ),
        cost_estimate=pl.CostEstimate(
            flops=14_000_000_000, bytes_accessed=12_000_000, transcendentals=17_000_000
        ),
    )(
        *(
            in_hbm(a)
            for a in (
                span_map.reshape(1, NE),
                branch_id.reshape(32, 128),
                derivative,
                couple.T,
                flux_weight.T,
                remap_cell,
                remap_weight,
                ocean_state,
                ocean_mask.reshape(4, 128),
                state,
                rad_weight,
                conv_in,
                conv_out,
            )
        ),
    )
    new_state, span_tend, ocean_new, surface = pl.pallas_call(
        place_kernel,
        out_shape=(
            out_hbm((ROWS, NF), BF16),
            out_hbm((ROWS, NF), BF16),
            out_hbm((2, 512), F32),
            out_hbm((2, ROWS), F32),
        ),
        in_specs=[smem] + [vmem] * 4,
        out_specs=(hbm,) * 4,
        scratch_shapes=[
            pltpu.VMEM((ROWS, NF), BF16),
            dma((4 + NE // PLACE,)),
        ],
        compiler_params=pltpu.CompilerParams(vmem_limit_bytes=8 << 20),
    )(
        pltpu.with_memory_space_constraint(places, pltpu.SMEM),
        *(stay(a) for a in (pool, new_state, ocean_new, surface)),
    )
    return new_state, span_tend, ocean_new, surface


def solution(mesh):
    cols = P(("atm", "ocn"), None)
    flat = P(("atm", "ocn"))
    lanes = P(None, ("atm", "ocn"))
    return jax.shard_map(
        body,
        mesh=mesh,
        in_specs=(cols, flat, flat, P(), P(), P(), P(), P(), lanes, lanes, lanes, flat, P()),
        out_specs=(cols, cols, lanes, lanes),
        check_vma=False,
    )
```
